32 devices in a mesh: scan: 8 (over z, y), mode: 4 (over x, core).
Axes of the slice: x: 2, y: 2, z: 4, core: 2. Of those that a mesh axis runs over, the one named last changes fastest.
Arguments:
- object_field: float32 [2, 512, 1024], P(None, 'scan', 'mode'), may hold values from -6 to 6
- probe: float32 [4, 2, 128, 128], P('mode'), may hold values from -6 to 6
- amplitude: float32 [64, 128, 128], P(('scan', 'mode')), may hold values from 0.5 to 8
- offsets: int32 [64, 2], P(('scan', 'mode')), may hold values from 0 to 1023, as said below
- counts: int32 [32], P(('scan', 'mode')), may hold values from 1 to 2, as said below
Outputs:
- object_out: float32 [2, 512, 1024], P(None, 'scan', 'mode')
- probe_out: float32 [4, 2, 128, 128], P('mode')
The draws below stay inside these ranges and needn't reach their ends.
Inputs may be any that keep to these rules, and one draw needn't show every extreme that they name: `offsets`: slot i belongs to the device of index i // 2 along scan+mode, with scan index s and mode index m; its top row lies in s * 64 to s * 64 + 63 and its left column in m * 256 to m * 256 + 255. `counts`: entry d is how many of the first slots of device d are used; some device uses all 2.
All inputs are finite; a program needn't handle non-finite values.
Results may differ from the reference program's by a relative error of at most 0.0001.
Values sent between devices are 32-bit elements; how exact they have to be, the bound alone decides.
No kernel may reach another device: no remote copies, remote signals or barrier semaphores. Data moves between devices by JAX's collectives and lax.ppermute only.
A program may use at most 64 MiB of HBM per device.

```python
import math
import jax
import jax.numpy as jnp
from jax import lax

P_SIZE = 128
TR = 64
BW = 256
POS_DEV = 2
ITERS = 2
MODES = 4
NO = 512
NC = 1024
NPOS = 64


def draw_offsets(key, part):
    key_row, key_col = jax.random.split(jax.random.fold_in(key, 11))
    slot_ids = jnp.arange(NPOS, dtype=jnp.int32)
    device_ids = slot_ids // POS_DEV
    band_count = NC // BW
    tile_ids = device_ids // band_count
    band_ids = device_ids % band_count
    row_start = tile_ids * TR + jax.random.randint(key_row, (NPOS,), 0, TR, dtype=jnp.int32)
    col_start = band_ids * BW + jax.random.randint(key_col, (NPOS,), 0, BW, dtype=jnp.int32)
    row_start = jnp.where(slot_ids == NPOS - 1, NO - 1, row_start)
    col_start = jnp.where(slot_ids == NPOS - 1, NC - 1, col_start)
    row_start = jnp.where(slot_ids == 0, 0, row_start)
    col_start = jnp.where(slot_ids == 0, 0, col_start)
    return jnp.stack([row_start, col_start], axis=1)


def draw_counts(key, part):
    key_count, key_full = jax.random.split(jax.random.fold_in(key, 23))
    group_total = NPOS // POS_DEV
    counts_drawn = jax.random.randint(key_count, (group_total,), 1, POS_DEV + 1, dtype=jnp.int32)
    chosen = jax.random.randint(key_full, (), 0, group_total, dtype=jnp.int32)
    return jnp.where(jnp.arange(group_total, dtype=jnp.int32) == chosen, POS_DEV, counts_drawn)


def levels(stream_key, dims, cuts, low, largest):
    gain = 1.0
    for axis_at, shards_of in cuts:
        heights = jax.random.uniform(jax.random.fold_in(jax.random.fold_in(stream_key, 6), axis_at), (shards_of,), jnp.float32, low / len(cuts), largest / len(cuts))
        gain = gain * jnp.repeat(jnp.exp(heights), dims[axis_at] // shards_of).reshape((-1,) + (1,) * (len(dims) - 1 - axis_at))
    return gain


def normal_values(stream_key, extent, deviation, bound, pieces=(), kind=jnp.bfloat16):
    drawn = jax.random.normal(stream_key, extent, jnp.float32) * deviation
    if len(pieces) > 0:
        drawn = levels(stream_key, extent, pieces, -0.22, 0.18) * drawn
    return jnp.clip(drawn, min=-bound, max=bound).astype(kind)


def setup_inputs(seed: int = 0) -> dict:
    key_of = jax.random.split(jax.random.key(seed), 6)
    return {
        "object_field": normal_values(key_of[0], (2, NO, NC), 1.0, 6.0, ((1, 8), (2, 4)), jnp.float32),
        "probe": normal_values(key_of[1], (MODES, 2, P_SIZE, P_SIZE), 1.0, 6.0, ((0, 4),), jnp.float32),
        "amplitude": jnp.clip(jnp.exp(math.log(8.0) - 2.7725887 * jax.random.uniform(key_of[2], (NPOS, P_SIZE, P_SIZE), jnp.float32) ** levels(key_of[2], (NPOS, P_SIZE, P_SIZE), ((0, 32),), -0.2, 0.2)), 0.5, 8.0),
        "offsets": draw_offsets(jax.random.fold_in(key_of[5], 71), 0),
        "counts": draw_counts(jax.random.fold_in(key_of[5], 71), 0),
    }


def fresnel_table(length):
    pixel_ids = jnp.arange(length, dtype=jnp.int32)
    phase_grid = pixel_ids[:, None] * pixel_ids[None, :] % length
    centred = pixel_ids - length // 2
    chirp = centred * centred % (4 * length)
    angle_table = -2.0 * math.pi / length * phase_grid.astype(jnp.float32) + math.pi / (2 * length) * chirp[None, :].astype(jnp.float32)
    factor = 1.0 / math.sqrt(length)
    return (jnp.cos(angle_table) * factor, jnp.sin(angle_table) * factor)

def product(form, first, second):
    return jnp.einsum(form, first, second, precision=lax.Precision.HIGHEST)

def wave_terms(object_patch, probes, amplitude_row, kern_re, kern_im):
    probe_re = probes[:, 0]
    probe_im = probes[:, 1]
    object_re = object_patch[0]
    object_im = object_patch[1]
    exit_re = probe_re * object_re - probe_im * object_im
    exit_im = probe_re * object_im + probe_im * object_re
    left_re = product('ux,kxy->kuy', kern_re, exit_re) - product('ux,kxy->kuy', kern_im, exit_im)
    left_im = product('ux,kxy->kuy', kern_re, exit_im) + product('ux,kxy->kuy', kern_im, exit_re)
    far_re = product('kuy,vy->kuv', left_re, kern_re) - product('kuy,vy->kuv', left_im, kern_im)
    far_im = product('kuy,vy->kuv', left_re, kern_im) + product('kuy,vy->kuv', left_im, kern_re)
    intensity = lax.optimization_barrier(jnp.sum(far_re * far_re + far_im * far_im, axis=0))
    factor = amplitude_row / jnp.sqrt(jnp.maximum(intensity, 1.0))
    fixed_re = far_re * factor
    fixed_im = far_im * factor
    back_re = product('ux,kuy->kxy', kern_re, fixed_re) + product('ux,kuy->kxy', kern_im, fixed_im)
    back_im = product('ux,kuy->kxy', kern_re, fixed_im) - product('ux,kuy->kxy', kern_im, fixed_re)
    near_re = product('kxv,vy->kxy', back_re, kern_re) + product('kxv,vy->kxy', back_im, kern_im)
    near_im = product('kxv,vy->kxy', back_im, kern_re) - product('kxv,vy->kxy', back_re, kern_im)
    change_re = near_re - exit_re
    change_im = near_im - exit_im
    numerator = jnp.stack([lax.optimization_barrier(jnp.sum(probe_re * change_re + probe_im * change_im, axis=0)), lax.optimization_barrier(jnp.sum(probe_re * change_im - probe_im * change_re, axis=0)), lax.optimization_barrier(jnp.sum(probe_re * probe_re + probe_im * probe_im, axis=0))])
    gradient = jnp.stack([object_re * change_re + object_im * change_im, object_re * change_im - object_im * change_re], axis=1)
    density = object_re * object_re + object_im * object_im
    return (numerator, gradient, density)

def reference(object_field, probe, amplitude, offsets, counts):
    kern_re, kern_im = fresnel_table(P_SIZE)
    slot_ids = jnp.arange(NPOS, dtype=jnp.int32)
    used_all = (slot_ids % POS_DEV < counts[slot_ids // POS_DEV]).astype(jnp.float32)
    start_zero = jnp.zeros((), jnp.int32)
    for iteration in range(ITERS):
        padded = jnp.pad(object_field, ((0, 0), (0, P_SIZE), (0, P_SIZE)))

        def add_position(slot, state_carry):
            sums, gradient, density = state_carry
            row_start = offsets[slot, 0].astype(jnp.int32)
            col_start = offsets[slot, 1].astype(jnp.int32)
            object_patch = lax.dynamic_slice(padded, (start_zero, row_start, col_start), (2, P_SIZE, P_SIZE))
            numerator, grad_term, dens_term = wave_terms(object_patch, probe, amplitude[slot], kern_re, kern_im)
            used = used_all[slot]
            current = lax.dynamic_slice(sums, (start_zero, row_start, col_start), (3, P_SIZE, P_SIZE))
            sums = lax.dynamic_update_slice(sums, current + used * numerator, (start_zero, row_start, col_start))
            return (sums, gradient + used * grad_term, density + used * dens_term)
        initial = (jnp.zeros((3, NO + P_SIZE, NC + P_SIZE), jnp.float32), jnp.zeros(probe.shape, jnp.float32), jnp.zeros((P_SIZE, P_SIZE), jnp.float32))
        sums, gradient, density = lax.fori_loop(0, NPOS, add_position, initial)
        object_new = object_field + sums[:2, :NO, :NC] / (sums[2:3, :NO, :NC] + 1.0)
        probe = probe + gradient / (density + 1.0)
        object_field = object_new
    return (object_field, probe)
```

```python
import functools
import math

import jax
import jax.numpy as jnp
import numpy as np
from jax import lax
from jax.experimental import pallas as pl
from jax.experimental.pallas import tpu as pltpu
from jax.sharding import PartitionSpec as P

ITERS = 2
SUBLANES, LANES = 8, 128
F32 = jnp.float32
BF16 = jnp.bfloat16


def shifted(value, axis, steps):
    count = lax.axis_size(axis)
    initial, last = (max(0, -steps), min(count, count - steps))
    return lax.ppermute(value, axis, [(source, source + steps) for source in range(initial, last)])


def swapped(value, axis, bit):
    return lax.ppermute(value, axis, [(i, i ^ bit) for i in range(lax.axis_size(axis))])


def bits_of(axis):
    return [1 << b for b in range(lax.axis_size(axis).bit_length() - 1)]


def gathered(value, axis):
    for bit in reversed(bits_of(axis)):
        value = jnp.concatenate([value, swapped(value, axis, bit)], axis=0)
    return value


def scattered(value, axis):
    for bit in bits_of(axis):
        half = value.shape[0] // 2
        value = value[:half] + swapped(value[half:], axis, bit)
    return value


def summed(value, axis):
    for bit in bits_of(axis):
        value = value + swapped(value, axis, bit)
    return value


@functools.lru_cache
def fresnel_parts(length):
    ids = np.arange(length, dtype=np.int64)
    phase = ids[:, None] * ids[None, :] % length
    centred = ids - length // 2
    chirp = centred * centred % (4 * length)
    angle = -2.0 * math.pi / length * phase + math.pi / (2 * length) * chirp[None, :]
    real, imag = np.cos(angle) / math.sqrt(length), np.sin(angle) / math.sqrt(length)
    whole = np.block([[real, -imag], [imag, real]])
    parts = []
    for matrix in (whole, whole.T):
        high = matrix.astype(jnp.bfloat16)
        low = (matrix - high.astype(np.float64)).astype(jnp.bfloat16)
        parts.append(np.stack([high, low]))
    return np.stack(parts)


def split(value):
    high = value.astype(BF16)
    return high, (value - high.astype(F32)).astype(BF16)


def dot(a, b):
    return jnp.dot(a, b, preferred_element_type=F32)


def window_of(row, col):
    return (
        pl.multiple_of(row // SUBLANES * SUBLANES, SUBLANES),
        pl.multiple_of(col // LANES * LANES, LANES),
        row % SUBLANES,
        col % LANES,
    )


def cut(wide, down, right, length):
    wide = pltpu.roll(wide, 2 * LANES - right, 1)[:, :length]
    return pltpu.roll(wide, length + SUBLANES - down, 0)[:length]


def placed_in(term, down, right):
    tall = jnp.concatenate([term, jnp.zeros((SUBLANES, term.shape[1]), F32)], axis=0)
    tall = pltpu.roll(tall, down, 0)
    return pltpu.roll(jnp.concatenate([tall, jnp.zeros_like(tall)], axis=1), right, 1)


def patches_kernel(place, extended, patch, density):
    slots, _, length, _ = patch.shape
    total = None
    for slot in range(slots):
        row, col, used = place[3 * slot], place[3 * slot + 1], place[3 * slot + 2]
        top, left, down, right = window_of(row, col)
        here = 0.0
        for part in range(2):
            wide = extended[part, pl.ds(top, length + SUBLANES), pl.ds(left, 2 * LANES)]
            window = cut(wide, down, right, length)
            patch[slot, part] = window
            here = here + window * window
        here = here * used.astype(F32)
        total = here if total is None else total + here
    density[...] = total


def wave_kernel(place, patch, probes, amplitude, table, sums, gradient, x_hi, x_lo, y_hi, y_lo, far):
    slots, _, length, _ = patch.shape
    modes = probes.shape[0]

    def from_left(which):
        for k in range(modes):
            cols = slice(k * length, (k + 1) * length)
            hi, lo = x_hi[:, cols], x_lo[:, cols]
            out = dot(table[which, 0], hi) + dot(table[which, 0], lo) + dot(table[which, 1], hi)
            hi, lo = split(out)
            rows = slice(k * length, (k + 1) * length)
            y_hi[rows, :length], y_hi[rows, length:] = hi[:length], hi[length:]
            y_lo[rows, :length], y_lo[rows, length:] = lo[:length], lo[length:]

    def from_right(which, k):
        rows = slice(k * length, (k + 1) * length)
        hi, lo = y_hi[rows], y_lo[rows]
        return dot(hi, table[which, 0]) + dot(lo, table[which, 0]) + dot(hi, table[which, 1])

    def set_columns(k, real, imag):
        cols = slice(k * length, (k + 1) * length)
        hi, lo = split(real)
        x_hi[:length, cols], x_lo[:length, cols] = hi, lo
        hi, lo = split(imag)
        x_hi[length:, cols], x_lo[length:, cols] = hi, lo

    sums[...] = jnp.zeros_like(sums)
    for slot in range(slots):
        row, col, used = place[3 * slot], place[3 * slot + 1], place[3 * slot + 2].astype(F32)
        obj_re, obj_im = patch[slot, 0], patch[slot, 1]
        for k in range(modes):
            pr, pi = probes[k, 0], probes[k, 1]
            set_columns(k, pr * obj_re - pi * obj_im, pr * obj_im + pi * obj_re)
        from_left(0)
        intensity = 0.0
        for k in range(modes):
            wave = from_right(1, k)
            far[k] = wave
            square = wave * wave
            intensity = intensity + square[:, :length] + square[:, length:]
        factor = amplitude[slot] / jnp.sqrt(jnp.maximum(intensity, 1.0))
        for k in range(modes):
            set_columns(k, far[k, :, :length] * factor, far[k, :, length:] * factor)
        from_left(1)
        num_re, num_im = 0.0, 0.0
        for k in range(modes):
            near = from_right(0, k)
            pr, pi = probes[k, 0], probes[k, 1]
            change_re = (near[:, :length] - (pr * obj_re - pi * obj_im)) * used
            change_im = (near[:, length:] - (pr * obj_im + pi * obj_re)) * used
            num_re = num_re + (pr * change_re + pi * change_im)
            num_im = num_im + (pr * change_im - pi * change_re)
            grad_re = obj_re * change_re + obj_im * change_im
            grad_im = obj_re * change_im - obj_im * change_re
            if slot == 0:
                gradient[k, 0], gradient[k, 1] = grad_re, grad_im
            else:
                gradient[k, 0] += grad_re
                gradient[k, 1] += grad_im
        top, left, down, right = window_of(row, col)
        for part, term in enumerate((num_re, num_im)):
            sums[part, pl.ds(top, length + SUBLANES), pl.ds(left, 2 * LANES)] += placed_in(term, down, right)


def weight_kernel(place, probes, weight, acc):
    modes, _, length, _ = probes.shape
    rows, cols = weight.shape
    top = acc.shape[0] - rows - length
    left = acc.shape[1] - cols - length
    power = 0.0
    for k in range(modes):
        power = power + (probes[k, 0] * probes[k, 0] + probes[k, 1] * probes[k, 1])
    acc[...] = jnp.zeros_like(acc)
    for slot in range(place.shape[0] // 3):
        row, col, used = place[3 * slot] + top, place[3 * slot + 1] + left, place[3 * slot + 2].astype(F32)
        above, before, down, right = window_of(row, col)
        acc[pl.ds(above, length + SUBLANES), pl.ds(before, 2 * LANES)] += placed_in(power * used, down, right)
    weight[...] = acc[pl.ds(top, rows), pl.ds(left, cols)]


VMEM = pl.BlockSpec(memory_space=pltpu.VMEM)
SMEM = pl.BlockSpec(memory_space=pltpu.SMEM)


def call(kernel, out_shape, in_specs, scratch=(), flops=0, moved=0):
    return pl.pallas_call(
        kernel,
        out_shape=out_shape,
        in_specs=in_specs,
        out_specs=jax.tree.map(lambda _: VMEM, out_shape),
        scratch_shapes=list(scratch),
        compiler_params=pltpu.CompilerParams(vmem_limit_bytes=32 * 2**20),
        cost_estimate=pl.CostEstimate(flops=flops, bytes_accessed=moved, transcendentals=0),
    )


def local(object_field, probe, amplitude, offsets, counts):
    tile_rows, band_cols = object_field.shape[1:]
    modes = lax.axis_size("mode")
    length = probe.shape[2]
    slots = amplitude.shape[0]
    reach = -(-length // tile_rows)
    ext_rows, ext_cols = tile_rows + length, band_cols + length
    table = jnp.asarray(fresnel_parts(length))
    used = (jnp.arange(slots, dtype=jnp.int32) < counts[0]).astype(jnp.int32)
    place = jnp.stack([offsets[:, 0] % tile_rows, offsets[:, 1] % band_cols, used], axis=1)

    before = jnp.stack([place, shifted(place, "mode", 1) - jnp.array([0, band_cols, 0], jnp.int32)])
    before = jnp.where(
        (lax.axis_index("mode") == 0) & (jnp.arange(2) == 1)[:, None, None], 0, before
    )
    windows = [before]
    for step in range(1, reach + 1):
        arrived = shifted(before, "scan", step) - jnp.array([step * tile_rows, 0, 0], jnp.int32)
        windows.append(jnp.where(lax.axis_index("scan") < step, 0, arrived))
    windows = jnp.concatenate(windows).reshape(-1)
    place = place.reshape(-1)

    def sds(*shape):
        return jax.ShapeDtypeStruct(shape, F32)

    wave_flops = slots * modes * 4 * 3 * 2 * 4 * length**3
    for iteration in range(ITERS):
        probes = gathered(probe, "mode")
        pieces = [object_field]
        for step in range(1, reach + 1):
            pieces.append(shifted(object_field, "scan", -step)[:, : length - (step - 1) * tile_rows])
        extended_rows = jnp.concatenate(pieces, axis=1)
        beside = shifted(extended_rows[:, :, :length], "mode", -1)
        extended = jnp.concatenate([extended_rows, beside], axis=2)
        patch, density = call(
            patches_kernel,
            (sds(slots, 2, length, length), sds(length, length)),
            [SMEM, VMEM],
            flops=2**20,
            moved=2**20,
        )(place, extended)
        sums, gradient = call(
            wave_kernel,
            (sds(2, ext_rows, ext_cols), sds(modes, 2, length, length)),
            [SMEM, VMEM, VMEM, VMEM, VMEM],
            [pltpu.VMEM((2 * length, modes * length), BF16)] * 2
            + [pltpu.VMEM((modes * length, 2 * length), BF16)] * 2
            + [pltpu.VMEM((modes, length, 2 * length), F32)],
            flops=wave_flops,
            moved=4 * 2**20,
        )(place, patch, probes, amplitude, table)
        weight = call(
            weight_kernel,
            sds(tile_rows, band_cols),
            [SMEM, VMEM],
            [pltpu.VMEM((reach * tile_rows + tile_rows + length, 2 * band_cols + length), F32)],
            flops=2**20,
            moved=2**20,
        )(windows, probes)
        density = summed(summed(density, "mode"), "scan")
        own = summed(scattered(gradient, "mode"), "scan")
        margin = shifted(sums[:, :, band_cols:], "mode", 1)
        folded = sums[:, :, :band_cols].at[:, :, :length].add(margin)
        block = folded[:, :tile_rows]
        for step in range(1, reach + 1):
            rows = folded[:, step * tile_rows : (step + 1) * tile_rows]
            arrived = shifted(rows, "scan", step)
            block = block.at[:, : arrived.shape[1]].add(arrived)
        object_field = object_field + block / (weight + 1.0)
        probe = probe + own / (density + 1.0)
    return (object_field, probe)


def solution(mesh):
    placed = (
        P(None, "scan", "mode"),
        P("mode", None, None, None),
        P(("scan", "mode"), None, None),
        P(("scan", "mode"), None),
        P(("scan", "mode")),
    )
    return jax.shard_map(
        local,
        mesh=mesh,
        in_specs=placed,
        out_specs=(P(None, "scan", "mode"), P("mode", None, None, None)),
        check_vma=False,
    )
```

```python
import functools
import math

import jax
import jax.numpy as jnp
import numpy as np
from jax import lax
from jax.experimental import pallas as pl
from jax.experimental.pallas import tpu as pltpu
from jax.sharding import PartitionSpec as P

ITERS = 2
SUBLANES, LANES = 8, 128
F32 = jnp.float32
BF16 = jnp.bfloat16
TABLE = 8


def shifted(value, axis, steps):
    count = lax.axis_size(axis)
    initial, last = (max(0, -steps), min(count, count - steps))
    return lax.ppermute(value, axis, [(source, source + steps) for source in range(initial, last)])


def swapped(value, axis, bit):
    return lax.ppermute(value, axis, [(i, i ^ bit) for i in range(lax.axis_size(axis))])


def paired(value, axis, step, phase):
    lower = [i for i in range(lax.axis_size(axis) - step) if i // step % 2 == phase]
    return lax.ppermute(value, axis, [(i, i + step) for i in lower] + [(i + step, i) for i in lower])


def across(value, scan_bit, mode_bit):
    scans, modes = lax.axis_size("scan"), lax.axis_size("mode")
    other = scan_bit * modes + mode_bit
    return lax.ppermute(value, ("scan", "mode"), [(i, i ^ other) for i in range(scans * modes)])


def bits_of(axis):
    return [1 << b for b in range(lax.axis_size(axis).bit_length() - 1)]


def gathered(value, axis):
    for bit in reversed(bits_of(axis)):
        value = jnp.concatenate([value, swapped(value, axis, bit)], axis=0)
    return value


@functools.lru_cache
def fresnel_parts(length):
    ids = np.arange(length, dtype=np.int64)
    phase = ids[:, None] * ids[None, :] % length
    centred = ids - length // 2
    chirp = centred * centred % (4 * length)
    angle = -2.0 * math.pi / length * phase + math.pi / (2 * length) * chirp[None, :]
    real, imag = np.cos(angle) / math.sqrt(length), np.sin(angle) / math.sqrt(length)
    whole = np.block([[real, -imag], [imag, real]])
    parts = []
    for matrix in (whole, whole.T):
        high = matrix.astype(jnp.bfloat16)
        low = (matrix - high.astype(np.float64)).astype(jnp.bfloat16)
        parts.append(np.stack([high, low]))
    return np.stack(parts)


def split(value):
    high = value.astype(BF16)
    return high, (value - high.astype(F32)).astype(BF16)


def dot(a, b):
    return jnp.dot(a, b, preferred_element_type=F32)


def window_of(row, col):
    return (
        pl.multiple_of(row // SUBLANES * SUBLANES, SUBLANES),
        pl.multiple_of(col // LANES * LANES, LANES),
        row % SUBLANES,
        col % LANES,
    )


def cut(wide, down, right, length):
    wide = pltpu.roll(wide, 2 * LANES - right, 1)[:, :length]
    return pltpu.roll(wide, length + SUBLANES - down, 0)[:length]


def placed_in(term, down, right):
    tall = jnp.concatenate([term, jnp.zeros((SUBLANES, term.shape[1]), F32)], axis=0)
    tall = pltpu.roll(tall, down, 0)
    return pltpu.roll(jnp.concatenate([tall, jnp.zeros_like(tall)], axis=1), right, 1)


def patches_kernel(place, first, second, third, patch, density, extended):
    slots, _, length, _ = patch.shape
    rows = first.shape[1]
    for step, tile in enumerate((first, second, third)):
        extended[:, step * rows : (step + 1) * rows] = tile[...]
    total = None
    for slot in range(slots):
        row, col, used = place[3 * slot], place[3 * slot + 1], place[3 * slot + 2]
        top, left, down, right = window_of(row, col)
        here = 0.0
        for part in range(2):
            wide = extended[part, pl.ds(top, length + SUBLANES), pl.ds(left, 2 * LANES)]
            window = cut(wide, down, right, length)
            patch[slot, part] = window
            here = here + window * window
        here = here * used.astype(F32)
        total = here if total is None else total + here
    density[...] = total


def whole_probe(probes, k, part, parity):
    return jnp.concatenate([probes[k, parity, part], probes[k, 1 - parity, part]], axis=0)


def wave_kernel(place, me, patch, density, probes, amplitude, table, windows, *rest):
    (kept, sent, *terms), (sums, x_hi, x_lo, y_hi, y_lo, far, own_probe) = rest[:-7], rest[-7:]
    slots, _, length, _ = patch.shape
    modes = probes.shape[0]
    half = length // 2
    scan = me[0]
    parity = scan % 2

    def from_left(which):
        for k in range(modes):
            cols = slice(k * length, (k + 1) * length)
            hi, lo = x_hi[:, cols], x_lo[:, cols]
            out = dot(table[which, 0], hi) + dot(table[which, 0], lo) + dot(table[which, 1], hi)
            hi, lo = split(out)
            rows = slice(k * length, (k + 1) * length)
            y_hi[rows, :length], y_hi[rows, length:] = hi[:length], hi[length:]
            y_lo[rows, :length], y_lo[rows, length:] = lo[:length], lo[length:]

    def from_right(which, k):
        rows = slice(k * length, (k + 1) * length)
        hi, lo = y_hi[rows], y_lo[rows]
        return dot(hi, table[which, 0]) + dot(lo, table[which, 0]) + dot(hi, table[which, 1])

    def set_columns(k, real, imag):
        cols = slice(k * length, (k + 1) * length)
        hi, lo = split(real)
        x_hi[:length, cols], x_lo[:length, cols] = hi, lo
        hi, lo = split(imag)
        x_hi[length:, cols], x_lo[length:, cols] = hi, lo

    sums[...] = jnp.zeros_like(sums)
    for k in range(modes):
        for part in range(2):
            own_probe[k, part] = whole_probe(probes, k, part, parity)
    for slot in range(slots):
        row, col, used = place[3 * slot], place[3 * slot + 1], place[3 * slot + 2].astype(F32)
        obj_re, obj_im = patch[slot, 0], patch[slot, 1]
        for k in range(modes):
            pr, pi = own_probe[k, 0], own_probe[k, 1]
            set_columns(k, pr * obj_re - pi * obj_im, pr * obj_im + pi * obj_re)
        from_left(0)
        intensity = 0.0
        for k in range(modes):
            wave = from_right(1, k)
            far[k] = wave
            square = wave * wave
            intensity = intensity + square[:, :length] + square[:, length:]
        factor = amplitude[slot] / jnp.sqrt(jnp.maximum(intensity, 1.0))
        for k in range(modes):
            set_columns(k, far[k, :, :length] * factor, far[k, :, length:] * factor)
        from_left(1)
        num_re, num_im = 0.0, 0.0
        for k in range(modes):
            near = from_right(0, k)
            pr, pi = own_probe[k, 0], own_probe[k, 1]
            change_re = (near[:, :length] - (pr * obj_re - pi * obj_im)) * used
            change_im = (near[:, length:] - (pr * obj_im + pi * obj_re)) * used
            num_re = num_re + (pr * change_re + pi * change_im)
            num_im = num_im + (pr * change_im - pi * change_re)
            grad_re = obj_re * change_re + obj_im * change_im
            grad_im = obj_re * change_im - obj_im * change_re
            out, at = (kept, k) if k < modes // 2 else (sent, k - modes // 2)
            for part, grad in enumerate((grad_re, grad_im)):
                for top in range(2):
                    where = (at, parity ^ top, slice(part * half, (part + 1) * half))
                    piece = grad[top * half : (top + 1) * half]
                    out[where] = piece if slot == 0 else out[where] + piece
        top, left, down, right = window_of(row, col)
        for part, term in enumerate((num_re, num_im)):
            sums[part, pl.ds(top, length + SUBLANES), pl.ds(left, 2 * LANES)] += placed_in(term, down, right)
    for out in (kept, sent):
        for at in range(modes // 2):
            for top in range(2):
                out[at, parity ^ top, 2 * half :] = density[top * half : (top + 1) * half]
    terms, rims = terms[:3], terms[3:]
    data_rows = terms[0].shape[0] - windows.shape[0]
    tile_rows = data_rows // 2
    for step, out in enumerate(terms):
        for part in range(2):
            out[part * tile_rows : (part + 1) * tile_rows] = sums[part, step * tile_rows : (step + 1) * tile_rows]
        out[data_rows:] = jnp.zeros((windows.shape[0], out.shape[1]), F32)
        out[data_rows:, LANES : 2 * LANES] = windows[...]
    for phase, rim in enumerate(rims):
        right = ((me[1] + phase) % 2 == 0).astype(jnp.int32)
        start = pl.multiple_of(right * (sums.shape[2] - length), LANES)
        for step in range(3):
            for part in range(2):
                at = (2 * step + part) * tile_rows
                rim[at : at + tile_rows] = sums[part, step * tile_rows : (step + 1) * tile_rows, pl.ds(start, length)]
        rim[3 * data_rows :] = windows[...]


def weight_of(table, me, probes, grid, scan_steps, mode_steps, rows, cols, tile_rows, band_cols, acc):
    modes, length = probes.shape[0], probes.shape[-1]
    above, left = (acc.shape[0] - rows - length, acc.shape[1] - cols - length)
    scan, mode = me[0], me[1]
    power = 0.0
    for k in range(modes):
        real, imag = (whole_probe(probes, k, part, scan % 2) for part in range(2))
        power = power + (real * real + imag * imag)
    acc[...] = jnp.zeros_like(acc)
    for ds in scan_steps:
        for dm in mode_steps:
            inside = (scan + ds >= 0) & (scan + ds < grid[0]) & (mode + dm >= 0) & (mode + dm < grid[1])
            first = jnp.where(inside, (scan + ds) * grid[1] + mode + dm, 0) * TABLE
            for slot in range(TABLE // 3):
                row = table[first + 3 * slot] - scan * tile_rows
                col = table[first + 3 * slot + 1] - mode * band_cols
                used = inside & (table[first + 3 * slot + 2] > 0)
                used &= (row > -length) & (row < rows) & (col > -length) & (col < cols)

                @pl.when(used)
                def _():
                    top, before, down, right = window_of(row + above, col + left)
                    acc[pl.ds(top, length + SUBLANES), pl.ds(before, 2 * LANES)] += placed_in(power, down, right)

    return acc[pl.ds(above, rows), pl.ds(left, cols)] + 1.0


def inner_kernel(grid, band_cols, table, me, first, third, probes, inner, outer, from_a, from_b, new_first, new_third, passed, acc):
    _, tile_rows, cols = first.shape
    scan, mode = me[0], me[1]
    weight = weight_of(
        table, me, probes, grid, range(-2, 3), range(-1, 2), 3 * tile_rows, cols, tile_rows, band_cols, acc
    )
    lower = (scan // 2 % 2 == 0).astype(F32)
    inside = jnp.where(lax.broadcasted_iota(jnp.int32, (tile_rows, cols), 1) < (grid[1] - mode) * band_cols, 1.0, 0.0)
    beyond = inside * (scan + 2 < grid[0]).astype(F32)
    is_first = (scan % 2).astype(F32)
    for part in range(2):
        rows = slice(part * tile_rows, (part + 1) * tile_rows)
        a, b = from_a[rows], from_b[rows]
        own = inner[rows] + (b * lower + a * (1.0 - lower))
        own = first[part] + inside * own / weight[:tile_rows]
        after = outer[rows] + (a * lower + b * (1.0 - lower))
        after = third[part] + beyond * after / weight[2 * tile_rows :]
        new_first[part], new_third[part] = own, after
        passed[part] = own * is_first + after * (1.0 - is_first)


def last_kernel(grid, table, me, probes, weight, acc):
    rows, cols = weight.shape
    weight[...] = weight_of(table, me, probes, grid, range(-2, 1), range(-1, 1), rows, cols, rows, cols, acc)


VMEM = pl.BlockSpec(memory_space=pltpu.VMEM)
SMEM = pl.BlockSpec(memory_space=pltpu.SMEM)


def call(kernel, out_shape, in_specs, scratch=(), flops=0, moved=0):
    return pl.pallas_call(
        kernel,
        out_shape=out_shape,
        in_specs=in_specs,
        out_specs=jax.tree.map(lambda _: VMEM, out_shape),
        scratch_shapes=list(scratch),
        compiler_params=pltpu.CompilerParams(vmem_limit_bytes=16 * 2**20),
        cost_estimate=pl.CostEstimate(flops=flops, bytes_accessed=moved, transcendentals=0),
    )


def local(object_field, probe, amplitude, offsets, counts):
    tile_rows, band_cols = object_field.shape[1:]
    scans, modes = lax.axis_size("scan"), lax.axis_size("mode")
    scan, mode = lax.axis_index("scan"), lax.axis_index("mode")
    length = probe.shape[2]
    slots = amplitude.shape[0]
    reach = -(-length // tile_rows)
    ext_rows, ext_cols = tile_rows + length, band_cols + length
    table = jnp.asarray(fresnel_parts(length))
    used = (jnp.arange(slots, dtype=jnp.int32) < counts[0]).astype(jnp.int32)
    corner = jnp.stack([scan * tile_rows, mode * band_cols]).astype(jnp.int32)
    place = jnp.concatenate([offsets - corner, used[:, None]], axis=1).reshape(-1)

    me = jnp.stack([scan, mode]).astype(jnp.int32)
    parity = scan % 2
    near, far = bits_of("mode")
    half = length // 2

    entry = jnp.concatenate([offsets, used[:, None]], axis=1).reshape(-1)
    entry = jnp.pad(entry, (0, TABLE - entry.shape[0])).astype(F32)
    table_rows = -(-scans * modes * TABLE // (SUBLANES * LANES)) * SUBLANES
    blocks = jnp.arange(table_rows * LANES // TABLE)
    windows = jnp.where((blocks == scan * modes + mode)[:, None], entry[None, :], 0.0).reshape(-1, LANES)
    data_rows = 2 * tile_rows
    even, odd = (parity == 0).astype(F32), (parity == 1).astype(F32)
    even_mode = (mode % 2 == 0).astype(F32)
    lower = (scan // 2 % 2 == 0).astype(F32)

    def sds(*shape):
        return jax.ShapeDtypeStruct(shape, F32)

    def as_halves(value):
        value = value.reshape(value.shape[0], 2, 2, half, length).swapaxes(1, 2)
        return jnp.where(parity == 0, value, value[:, ::-1])

    def scratch(rows, cols):
        return [pltpu.VMEM((reach * tile_rows + rows + length, band_cols + cols + length), F32)]

    def inner_update(first, third, probes, terms, rims):
        a, b = (paired(rim, "mode", 1, phase) for phase, rim in enumerate(rims))
        left, right = b * even_mode + a * (1.0 - even_mode), a * even_mode + b * (1.0 - even_mode)
        joined = []
        for step, term in enumerate(terms):
            rows = slice(step * data_rows, (step + 1) * data_rows)
            parts = [term[:data_rows, :length] + left[rows], term[:data_rows, length:band_cols], term[:data_rows, band_cols:] + right[rows]]
            joined.append(jnp.concatenate(parts, axis=1))
        here = terms[0][data_rows:, LANES : 2 * LANES] + (a + b)[3 * data_rows :]
        here = jnp.pad(here, ((0, 0), (0, ext_cols - LANES)))
        arrived = swapped(jnp.concatenate([joined[1], here]), "scan", 1)
        entries = here + arrived[data_rows:]
        inner = joined[0] + arrived[:data_rows] * odd
        outer = joined[2] + arrived[:data_rows] * even
        a = paired(jnp.concatenate([outer * lower + inner * (1.0 - lower), entries]), "scan", 2, 0)
        b = paired(jnp.concatenate([inner * lower + outer * (1.0 - lower), entries]), "scan", 2, 1)
        entries = (entries + a[data_rows:] + b[data_rows:])[:, :LANES].astype(jnp.int32).reshape(-1)
        first, third, passed = call(
            functools.partial(inner_kernel, (scans, modes), band_cols),
            [sds(2, tile_rows, ext_cols)] * 3,
            [SMEM, SMEM] + [VMEM] * 7,
            scratch(3 * tile_rows, ext_cols),
            flops=2**20,
            moved=2**20,
        )(entries, me, first, third, probes, inner, outer, a, b)
        return first, third, passed, entries

    def last_update(tile, probes, terms, entries):
        arrived = swapped(terms[1][:data_rows], "scan", 1)
        third = terms[2][:data_rows] + arrived * even
        first = terms[0][:data_rows] + arrived * odd + shifted(third, "scan", 2)
        return first

    def last_part(tile, probes, first, entries):
        weight = call(
            functools.partial(last_kernel, (scans, modes)),
            sds(tile_rows, band_cols),
            [SMEM, SMEM, VMEM],
            scratch(tile_rows, band_cols),
            flops=2**20,
            moved=2**20,
        )(entries, me, probes)
        margin = shifted(first[:, band_cols:], "mode", 1)
        terms = jnp.concatenate([first[:, :length] + margin, first[:, length:band_cols]], axis=1)
        return tile[:, :, :band_cols] + terms.reshape(2, tile_rows, band_cols) / weight

    probes = gathered(as_halves(probe), "mode")
    tiles = [object_field, shifted(object_field, "scan", -1), shifted(object_field, "scan", -2)]
    tiles = jnp.concatenate(tiles, axis=1)
    tiles = jnp.concatenate([tiles, shifted(tiles[:, :, :length], "mode", -1)], axis=2)
    first, second, third = (tiles[:, step * tile_rows : (step + 1) * tile_rows] for step in range(3))
    for iteration in range(ITERS):
        last = iteration == ITERS - 1
        patch, density = call(
            patches_kernel,
            (sds(slots, 2, length, length), sds(length, length)),
            [SMEM] + [VMEM] * 3,
            [pltpu.VMEM((2, ext_rows, ext_cols), F32)],
            flops=2**20,
            moved=2**20,
        )(place, first, second, third)
        rows_out = data_rows + table_rows
        kept, sent, *terms = call(
            wave_kernel,
            (*[sds(modes // 2, 2, 3 * half, length)] * 2, *[sds(rows_out, ext_cols)] * 3, *[sds(2 * data_rows + rows_out, length)] * (0 if last else 2)),
            [SMEM, SMEM] + [VMEM] * 6,
            [pltpu.VMEM((2, ext_rows, ext_cols), F32)]
            + [pltpu.VMEM((2 * length, modes * length), BF16)] * 2
            + [pltpu.VMEM((modes * length, 2 * length), BF16)] * 2
            + [pltpu.VMEM((modes, length, 2 * length), F32), pltpu.VMEM((modes, 2, length, length), F32)],
            flops=slots * modes * 4 * 3 * 2 * 4 * length**3,
            moved=4 * 2**20,
        )(place, me, patch, density, probes, amplitude, table, windows)
        kept = kept + swapped(sent, "mode", near)
        if last:
            kept, terms = lax.optimization_barrier((kept, terms))
        own = kept[0, 0] + across(kept[0, 1], 1, 0) + across(kept[1, 0], 0, far) + across(kept[1, 1], 1, far)
        for bit in bits_of("scan")[1:]:
            own = own + swapped(own, "scan", bit)
        if not last:
            first, third, passed, entries = inner_update(first, third, probes, terms[:3], terms[3:])
            own, passed = lax.optimization_barrier((own, passed))
        else:
            inner = last_update(first, probes, terms[:3], entries)
            own, inner = lax.optimization_barrier((own, inner))
        probe = probes[0, 0] + own[: 2 * half].reshape(2, half, length) / (own[2 * half :] + 1.0)
        if not last:
            second = swapped(passed, "scan", 1)
            probes = jnp.stack(
                [
                    jnp.stack([probe, across(probe, 1, 0)]),
                    jnp.stack([across(probe, 0, far), across(probe, 1, far)]),
                ]
            )
            probes, second = lax.optimization_barrier((probes, second))
            probes = jnp.concatenate([probes, swapped(probes, "mode", near)], axis=0)
        else:
            object_field = last_part(first, probes, inner, entries)
            probe = jnp.stack([probe, across(probe, 1, 0)])
            probe = jnp.where(parity == 0, probe, probe[::-1]).swapaxes(0, 1).reshape(1, 2, length, length)
    return (object_field, probe)


def solution(mesh):
    placed = (
        P(None, "scan", "mode"),
        P("mode", None, None, None),
        P(("scan", "mode"), None, None),
        P(("scan", "mode"), None),
        P(("scan", "mode")),
    )
    return jax.shard_map(
        local,
        mesh=mesh,
        in_specs=placed,
        out_specs=(P(None, "scan", "mode"), P("mode", None, None, None)),
        check_vma=False,
    )
```

```python
import functools
import math

import jax
import jax.numpy as jnp
import numpy as np
from jax import lax
from jax.experimental import pallas as pl
from jax.experimental.pallas import tpu as pltpu
from jax.sharding import PartitionSpec as P

ITERS = 2
SUBLANES, LANES = 8, 128
F32 = jnp.float32
BF16 = jnp.bfloat16
TABLE = 8


def shifted(value, axis, steps):
    count = lax.axis_size(axis)
    initial, last = (max(0, -steps), min(count, count - steps))
    return lax.ppermute(value, axis, [(source, source + steps) for source in range(initial, last)])


def swapped(value, axis, bit):
    return lax.ppermute(value, axis, [(i, i ^ bit) for i in range(lax.axis_size(axis))])


def paired(value, axis, step, phase):
    lower = [i for i in range(lax.axis_size(axis) - step) if i // step % 2 == phase]
    return lax.ppermute(value, axis, [(i, i + step) for i in lower] + [(i + step, i) for i in lower])


def across(value, scan_bit, mode_bit):
    scans, modes = lax.axis_size("scan"), lax.axis_size("mode")
    other = scan_bit * modes + mode_bit
    return lax.ppermute(value, ("scan", "mode"), [(i, i ^ other) for i in range(scans * modes)])


def after(value, others):
    return lax.optimization_barrier((value, others))[0]


def bits_of(axis):
    return [1 << b for b in range(lax.axis_size(axis).bit_length() - 1)]


def gathered(value, axis):
    for bit in reversed(bits_of(axis)):
        value = jnp.concatenate([value, swapped(value, axis, bit)], axis=0)
    return value


@functools.lru_cache
def fresnel_parts(length):
    ids = np.arange(length, dtype=np.int64)
    phase = ids[:, None] * ids[None, :] % length
    centred = ids - length // 2
    chirp = centred * centred % (4 * length)
    angle = -2.0 * math.pi / length * phase + math.pi / (2 * length) * chirp[None, :]
    real, imag = np.cos(angle) / math.sqrt(length), np.sin(angle) / math.sqrt(length)
    whole = np.block([[real, -imag], [imag, real]])
    parts = []
    for matrix in (whole, whole.T):
        high = matrix.astype(jnp.bfloat16)
        low = (matrix - high.astype(np.float64)).astype(jnp.bfloat16)
        parts.append(np.stack([high, low]))
    return np.stack(parts)


def split(value):
    high = value.astype(BF16)
    return high, (value - high.astype(F32)).astype(BF16)


def dot(a, b):
    return jnp.dot(a, b, preferred_element_type=F32)


def window_of(row, col):
    return (
        pl.multiple_of(row // SUBLANES * SUBLANES, SUBLANES),
        pl.multiple_of(col // LANES * LANES, LANES),
        row % SUBLANES,
        col % LANES,
    )


def cut(wide, down, right, length):
    wide = pltpu.roll(wide, 2 * LANES - right, 1)[:, :length]
    return pltpu.roll(wide, length + SUBLANES - down, 0)[:length]


def placed_in(term, down, right):
    tall = jnp.concatenate([term, jnp.zeros((SUBLANES, term.shape[1]), F32)], axis=0)
    tall = pltpu.roll(pltpu.roll(tall, down, 0), right, 1)
    first = lax.broadcasted_iota(jnp.int32, tall.shape, 1) >= right
    return jnp.concatenate([jnp.where(first, tall, 0.0), jnp.where(first, 0.0, tall)], axis=1)


def patches_kernel(place, first, second, third, patch, density, extended):
    slots, _, length, _ = patch.shape
    rows = first.shape[1]
    for step, tile in enumerate((first, second, third)):
        extended[:, step * rows : (step + 1) * rows] = tile[...]
    total = None
    for slot in range(slots):
        row, col, used = place[3 * slot], place[3 * slot + 1], place[3 * slot + 2]
        top, left, down, right = window_of(row, col)
        here = 0.0
        for part in range(2):
            wide = extended[part, pl.ds(top, length + SUBLANES), pl.ds(left, 2 * LANES)]
            window = cut(wide, down, right, length)
            patch[slot, part] = window
            here = here + window * window
        here = here * used.astype(F32)
        total = here if total is None else total + here
    density[...] = total


def whole_probe(probes, k, part, parity):
    return jnp.concatenate([probes[k, parity, part], probes[k, 1 - parity, part]], axis=0)


def wave_kernel(place, me, patch, density, probes, amplitude, table, windows, *rest):
    (kept, sent, *terms), (sums, x_hi, x_lo, y_hi, y_lo, far, own_probe) = rest[:-7], rest[-7:]
    slots, _, length, _ = patch.shape
    modes = probes.shape[0]
    half = length // 2
    scan = me[0]
    parity = scan % 2

    def from_left(which):
        for pair in range(modes // 2):
            cols = slice(2 * pair * length, 2 * (pair + 1) * length)
            hi, lo = x_hi[:, cols], x_lo[:, cols]
            out = dot(table[which, 0], hi) + dot(table[which, 0], lo) + dot(table[which, 1], hi)
            hi, lo = split(out)
            for k in range(2):
                rows = slice((2 * pair + k) * length, (2 * pair + k + 1) * length)
                cols = slice(k * length, (k + 1) * length)
                y_hi[rows, :length], y_hi[rows, length:] = hi[:length, cols], hi[length:, cols]
                y_lo[rows, :length], y_lo[rows, length:] = lo[:length, cols], lo[length:, cols]

    def from_right(which, k):
        rows = slice(k * length, (k + 1) * length)
        hi, lo = y_hi[rows], y_lo[rows]
        return dot(hi, table[which, 0]) + dot(lo, table[which, 0]) + dot(hi, table[which, 1])

    def set_columns(k, real, imag):
        cols = slice(k * length, (k + 1) * length)
        hi, lo = split(real)
        x_hi[:length, cols], x_lo[:length, cols] = hi, lo
        hi, lo = split(imag)
        x_hi[length:, cols], x_lo[length:, cols] = hi, lo

    sums[...] = jnp.zeros_like(sums)
    for k in range(modes):
        for part in range(2):
            own_probe[k, part] = whole_probe(probes, k, part, parity)
    for slot in range(slots):
        row, col, used = place[3 * slot], place[3 * slot + 1], place[3 * slot + 2].astype(F32)
        obj_re, obj_im = patch[slot, 0], patch[slot, 1]
        for k in range(modes):
            pr, pi = own_probe[k, 0], own_probe[k, 1]
            set_columns(k, pr * obj_re - pi * obj_im, pr * obj_im + pi * obj_re)
        from_left(0)
        intensity = 0.0
        for k in range(modes):
            wave = from_right(1, k)
            far[k] = wave
            square = wave * wave
            intensity = intensity + square[:, :length] + square[:, length:]
        factor = amplitude[slot] / jnp.sqrt(jnp.maximum(intensity, 1.0))
        for k in range(modes):
            set_columns(k, far[k, :, :length] * factor, far[k, :, length:] * factor)
        from_left(1)
        num_re, num_im = 0.0, 0.0
        for k in range(modes):
            near = from_right(0, k)
            pr, pi = own_probe[k, 0], own_probe[k, 1]
            change_re = (near[:, :length] - (pr * obj_re - pi * obj_im)) * used
            change_im = (near[:, length:] - (pr * obj_im + pi * obj_re)) * used
            num_re = num_re + (pr * change_re + pi * change_im)
            num_im = num_im + (pr * change_im - pi * change_re)
            grad_re = obj_re * change_re + obj_im * change_im
            grad_im = obj_re * change_im - obj_im * change_re
            out, at = (kept, k) if k < modes // 2 else (sent, k - modes // 2)
            for part, grad in enumerate((grad_re, grad_im)):
                for top in range(2):
                    where = (at, parity ^ top, slice(part * half, (part + 1) * half))
                    piece = grad[top * half : (top + 1) * half]
                    out[where] = piece if slot == 0 else out[where] + piece
        top, left, down, right = window_of(row, col)
        for part, term in enumerate((num_re, num_im)):
            sums[part, pl.ds(top, length + SUBLANES), pl.ds(left, 2 * LANES)] += placed_in(term, down, right)
    for out in (kept, sent):
        for at in range(modes // 2):
            for top in range(2):
                out[at, parity ^ top, 2 * half :] = density[top * half : (top + 1) * half]
    data_rows = terms[0].shape[0] - windows.shape[0]
    tile_rows = data_rows // 2
    for step, out in enumerate(terms):
        for part in range(2):
            out[part * tile_rows : (part + 1) * tile_rows] = sums[part, step * tile_rows : (step + 1) * tile_rows]
        out[data_rows:] = jnp.zeros((windows.shape[0], out.shape[1]), F32)
        out[data_rows:, LANES : 2 * LANES] = windows[...]


def weight_of(table, me, probes, grid, scan_steps, mode_steps, rows, cols, tile_rows, band_cols, acc):
    modes, length = probes.shape[0], probes.shape[-1]
    above, left = (acc.shape[0] - rows - length, acc.shape[1] - cols - length)
    scan, mode = me[0], me[1]
    power = 0.0
    for k in range(modes):
        real, imag = (whole_probe(probes, k, part, scan % 2) for part in range(2))
        power = power + (real * real + imag * imag)
    acc[...] = jnp.zeros_like(acc)
    for ds in scan_steps:
        for dm in mode_steps:
            inside = (scan + ds >= 0) & (scan + ds < grid[0]) & (mode + dm >= 0) & (mode + dm < grid[1])
            first = jnp.where(inside, (scan + ds) * grid[1] + mode + dm, 0) * TABLE
            for slot in range(TABLE // 3):
                row = table[first + 3 * slot] - scan * tile_rows
                col = table[first + 3 * slot + 1] - mode * band_cols
                used = inside & (table[first + 3 * slot + 2] > 0)
                used &= (row > -length) & (row < rows) & (col > -length) & (col < cols)

                @pl.when(used)
                def _():
                    top, before, down, right = window_of(row + above, col + left)
                    acc[pl.ds(top, length + SUBLANES), pl.ds(before, 2 * LANES)] += placed_in(power, down, right)

    return acc[pl.ds(above, rows), pl.ds(left, cols)] + 1.0


def join_kernel(band_cols, me, inner, outer, entries, from_a, from_b, new_inner, new_outer, for_a, for_b):
    data_rows = inner.shape[0]
    rim = for_a.shape[1]
    lower = (me[0] // 2 % 2 == 0).astype(F32)
    even = (me[1] % 2 == 0).astype(F32)
    a, b = from_a[:data_rows], from_b[:data_rows]
    tiles = (inner[...] + b * lower + a * (1.0 - lower), outer[...] + a * lower + b * (1.0 - lower))
    new_inner[...], new_outer[...] = tiles
    for at, tile in enumerate(tiles):
        rows = slice(at * data_rows, (at + 1) * data_rows)
        left, right = tile[:, :rim], tile[:, band_cols:]
        for_a[rows] = right * even + left * (1.0 - even)
        for_b[rows] = left * even + right * (1.0 - even)
    rest = entries[...] + from_a[data_rows:, LANES : 2 * LANES] + from_b[data_rows:, LANES : 2 * LANES]
    for_a[2 * data_rows :] = rest
    for_b[2 * data_rows :] = rest


def inner_kernel(grid, band_cols, table, me, first, third, probes, inner, outer, from_a, from_b, new_first, new_third, passed, acc):
    _, tile_rows, cols = first.shape
    rim = from_a.shape[1]
    scan, mode = me[0], me[1]
    weight = weight_of(
        table, me, probes, grid, range(-2, 3), range(-1, 2), 3 * tile_rows, cols, tile_rows, band_cols, acc
    )
    inside = jnp.where(lax.broadcasted_iota(jnp.int32, (tile_rows, cols), 1) < (grid[1] - mode) * band_cols, 1.0, 0.0)
    beyond = inside * (scan + 2 < grid[0]).astype(F32)
    is_first = (scan % 2).astype(F32)
    even = (mode % 2 == 0).astype(F32)
    for part in range(2):
        updated = []
        for at, (term, tile, keep) in enumerate(((inner, first, inside), (outer, third, beyond))):
            a, b = (ref[slice((2 * at + part) * tile_rows, (2 * at + part + 1) * tile_rows)] for ref in (from_a, from_b))
            left, right = b * even + a * (1.0 - even), a * even + b * (1.0 - even)
            term = term[part * tile_rows : (part + 1) * tile_rows]
            term = jnp.concatenate([term[:, :rim] + left, term[:, rim:band_cols], term[:, band_cols:] + right], axis=1)
            updated.append(tile[part] + keep * term / weight[2 * at * tile_rows : (2 * at + 1) * tile_rows])
        new_first[part], new_third[part] = updated
        passed[part] = updated[0] * is_first + updated[1] * (1.0 - is_first)


def last_kernel(grid, table, me, probes, weight, acc):
    rows, cols = weight.shape
    weight[...] = weight_of(table, me, probes, grid, range(-2, 1), range(-1, 1), rows, cols, rows, cols, acc)


VMEM = pl.BlockSpec(memory_space=pltpu.VMEM)
SMEM = pl.BlockSpec(memory_space=pltpu.SMEM)


def call(kernel, out_shape, in_specs, scratch=(), flops=0, moved=0):
    return pl.pallas_call(
        kernel,
        out_shape=out_shape,
        in_specs=in_specs,
        out_specs=jax.tree.map(lambda _: VMEM, out_shape),
        scratch_shapes=list(scratch),
        compiler_params=pltpu.CompilerParams(vmem_limit_bytes=16 * 2**20),
        cost_estimate=pl.CostEstimate(flops=flops, bytes_accessed=moved, transcendentals=0),
    )


def local(object_field, probe, amplitude, offsets, counts):
    tile_rows, band_cols = object_field.shape[1:]
    scans, modes = lax.axis_size("scan"), lax.axis_size("mode")
    scan, mode = lax.axis_index("scan"), lax.axis_index("mode")
    length = probe.shape[2]
    slots = amplitude.shape[0]
    reach = -(-length // tile_rows)
    ext_rows, ext_cols = tile_rows + length, band_cols + length
    table = jnp.asarray(fresnel_parts(length))
    used = (jnp.arange(slots, dtype=jnp.int32) < counts[0]).astype(jnp.int32)
    corner = jnp.stack([scan * tile_rows, mode * band_cols]).astype(jnp.int32)
    place = jnp.concatenate([offsets - corner, used[:, None]], axis=1).reshape(-1)

    me = jnp.stack([scan, mode]).astype(jnp.int32)
    parity = scan % 2
    near, far = bits_of("mode")
    half = length // 2

    entry = jnp.concatenate([offsets, used[:, None]], axis=1).reshape(-1)
    entry = jnp.pad(entry, (0, TABLE - entry.shape[0])).astype(F32)
    table_rows = -(-scans * modes * TABLE // (SUBLANES * LANES)) * SUBLANES
    blocks = jnp.arange(table_rows * LANES // TABLE)
    windows = jnp.where((blocks == scan * modes + mode)[:, None], entry[None, :], 0.0).reshape(-1, LANES)
    data_rows = 2 * tile_rows
    even, odd = (parity == 0).astype(F32), (parity == 1).astype(F32)
    even_mode = (mode % 2 == 0).astype(F32)
    lower = (scan // 2 % 2 == 0).astype(F32)

    def sds(*shape):
        return jax.ShapeDtypeStruct(shape, F32)

    def as_halves(value):
        value = value.reshape(value.shape[0], 2, 2, half, length).swapaxes(1, 2)
        return jnp.where(parity == 0, value, value[:, ::-1])

    def scratch(rows, cols):
        return [pltpu.VMEM((reach * tile_rows + rows + length, band_cols + cols + length), F32)]

    def joined_rows(terms):
        arrived = swapped(terms[1], "scan", 1)
        inner = terms[0][:data_rows] + arrived[:data_rows] * odd
        outer = terms[2][:data_rows] + arrived[:data_rows] * even
        entries = terms[0][data_rows:] + arrived[data_rows:]
        a = paired(jnp.concatenate([outer * lower + inner * (1.0 - lower), entries]), "scan", 2, 0)
        b = paired(jnp.concatenate([inner * lower + outer * (1.0 - lower), entries]), "scan", 2, 1)
        rows = 2 * data_rows + table_rows
        return call(
            functools.partial(join_kernel, band_cols),
            [sds(data_rows, ext_cols)] * 2 + [sds(rows, length)] * 2,
            [SMEM] + [VMEM] * 5,
            flops=2**20,
            moved=2**20,
        )(me, inner, outer, entries[:, LANES : 2 * LANES], a, b)

    def inner_update(first, third, probes, inner, outer, for_a, for_b):
        a, b = paired(for_a, "mode", 1, 0), paired(for_b, "mode", 1, 1)
        entries = (for_a + a + b)[2 * data_rows :].astype(jnp.int32).reshape(-1)
        first, third, passed = call(
            functools.partial(inner_kernel, (scans, modes), band_cols),
            [sds(2, tile_rows, ext_cols)] * 3,
            [SMEM, SMEM] + [VMEM] * 7,
            scratch(3 * tile_rows, ext_cols),
            flops=2**20,
            moved=2**20,
        )(entries, me, first, third, probes, inner, outer, a, b)
        return first, third, passed, entries

    def last_update(tile, probes, terms, entries):
        arrived = swapped(terms[1][:data_rows], "scan", 1)
        third = terms[2][:data_rows] + arrived * even
        first = terms[0][:data_rows] + arrived * odd + shifted(third, "scan", 2)
        return first

    def last_part(tile, probes, first, entries):
        weight = call(
            functools.partial(last_kernel, (scans, modes)),
            sds(tile_rows, band_cols),
            [SMEM, SMEM, VMEM],
            scratch(tile_rows, band_cols),
            flops=2**20,
            moved=2**20,
        )(entries, me, probes)
        margin = shifted(first[:, band_cols:], "mode", 1)
        terms = jnp.concatenate([first[:, :length] + margin, first[:, length:band_cols]], axis=1)
        return tile[:, :, :band_cols] + terms.reshape(2, tile_rows, band_cols) / weight

    probes = as_halves(probe)
    probes = jnp.concatenate([probes, swapped(probes, "mode", far)], axis=0)
    tiles = [object_field, shifted(object_field, "scan", -1), shifted(object_field, "scan", -2)]
    tiles = jnp.concatenate(tiles, axis=1)
    tiles = jnp.concatenate([tiles, shifted(tiles[:, :, :length], "mode", -1)], axis=2)
    probes = after(probes, tiles)
    probes = jnp.concatenate([probes, swapped(probes, "mode", near)], axis=0)
    first, second, third = (tiles[:, step * tile_rows : (step + 1) * tile_rows] for step in range(3))
    for iteration in range(ITERS):
        last = iteration == ITERS - 1
        patch, density = call(
            patches_kernel,
            (sds(slots, 2, length, length), sds(length, length)),
            [SMEM] + [VMEM] * 3,
            [pltpu.VMEM((2, ext_rows, ext_cols), F32)],
            flops=2**20,
            moved=2**20,
        )(place, first, second, third)
        rows_out = data_rows + table_rows
        kept, sent, *terms = call(
            wave_kernel,
            (*[sds(modes // 2, 2, 3 * half, length)] * 2, *[sds(rows_out, ext_cols)] * 3),
            [SMEM, SMEM] + [VMEM] * 6,
            [pltpu.VMEM((2, ext_rows, ext_cols), F32)]
            + [pltpu.VMEM((2 * length, modes * length), BF16)] * 2
            + [pltpu.VMEM((modes * length, 2 * length), BF16)] * 2
            + [pltpu.VMEM((modes, length, 2 * length), F32), pltpu.VMEM((modes, 2, length, length), F32)],
            flops=slots * modes * 4 * 3 * 2 * 4 * length**3,
            moved=4 * 2**20,
        )(place, me, patch, density, probes, amplitude, table, windows)
        kept = kept + swapped(sent, "mode", near)
        if last:
            kept, terms = lax.optimization_barrier((kept, terms))
        pass
        own = kept[0, 0] + across(kept[0, 1], 1, 0) + across(kept[1, 0], 0, far) + across(kept[1, 1], 1, far)
        if not last:
            joined = joined_rows(terms)
        pass
        for bit in bits_of("scan")[1:]:
            own = own + swapped(own, "scan", bit)
            pass
        if not last:
            first, third, passed, entries = inner_update(first, third, probes, *joined)
            own = after(own, passed)
        else:
            inner = last_update(first, probes, terms[:3], entries)
            own = after(own, inner)
        probe = probes[0, 0] + own[: 2 * half].reshape(2, half, length) / (own[2 * half :] + 1.0)
        if not last:
            second = swapped(passed, "scan", 1)
            probes = jnp.stack(
                [
                    jnp.stack([probe, across(probe, 1, 0)]),
                    jnp.stack([across(probe, 0, far), across(probe, 1, far)]),
                ]
            )
            probes = after(probes, second)
            probes = jnp.concatenate([probes, swapped(probes, "mode", near)], axis=0)
        else:
            object_field = last_part(first, probes, inner, entries)
            probe = jnp.stack([probe, across(probe, 1, 0)])
            probe = jnp.where(parity == 0, probe, probe[::-1]).swapaxes(0, 1).reshape(1, 2, length, length)
    return (object_field, probe)


def solution(mesh):
    placed = (
        P(None, "scan", "mode"),
        P("mode", None, None, None),
        P(("scan", "mode"), None, None),
        P(("scan", "mode"), None),
        P(("scan", "mode")),
    )
    return jax.shard_map(
        local,
        mesh=mesh,
        in_specs=placed,
        out_specs=(P(None, "scan", "mode"), P("mode", None, None, None)),
        check_vma=False,
    )
```

```python
import functools
import math

import jax
import jax.numpy as jnp
import numpy as np
from jax import lax
from jax.experimental import pallas as pl
from jax.experimental.pallas import tpu as pltpu
from jax.sharding import PartitionSpec as P

ITERS = 2
SUBLANES, LANES = 8, 128
F32 = jnp.float32
BF16 = jnp.bfloat16
TABLE = 8


def shifted(value, axis, steps):
    count = lax.axis_size(axis)
    initial, last = (max(0, -steps), min(count, count - steps))
    return lax.ppermute(value, axis, [(source, source + steps) for source in range(initial, last)])


def swapped(value, axis, bit):
    return lax.ppermute(value, axis, [(i, i ^ bit) for i in range(lax.axis_size(axis))])


def paired(value, axis, step, phase):
    lower = [i for i in range(lax.axis_size(axis) - step) if i // step % 2 == phase]
    return lax.ppermute(value, axis, [(i, i + step) for i in lower] + [(i + step, i) for i in lower])


def across(value, scan_bit, mode_bit):
    scans, modes = lax.axis_size("scan"), lax.axis_size("mode")
    other = scan_bit * modes + mode_bit
    return lax.ppermute(value, ("scan", "mode"), [(i, i ^ other) for i in range(scans * modes)])


def after(value, others):
    return lax.optimization_barrier((value, others))[0]


def bits_of(axis):
    return [1 << b for b in range(lax.axis_size(axis).bit_length() - 1)]


def gathered(value, axis):
    for bit in reversed(bits_of(axis)):
        value = jnp.concatenate([value, swapped(value, axis, bit)], axis=0)
    return value


@functools.lru_cache
def fresnel_parts(length):
    ids = np.arange(length, dtype=np.int64)
    phase = ids[:, None] * ids[None, :] % length
    centred = ids - length // 2
    chirp = centred * centred % (4 * length)
    angle = -2.0 * math.pi / length * phase + math.pi / (2 * length) * chirp[None, :]
    real, imag = np.cos(angle) / math.sqrt(length), np.sin(angle) / math.sqrt(length)
    whole = np.block([[real, -imag], [imag, real]])
    parts = []
    for matrix in (whole, whole.T):
        high = matrix.astype(jnp.bfloat16)
        low = (matrix - high.astype(np.float64)).astype(jnp.bfloat16)
        parts.append(np.stack([high, low]))
    return np.stack(parts)


def split(value):
    high = value.astype(BF16)
    return high, (value - high.astype(F32)).astype(BF16)


def dot(a, b):
    return jnp.dot(a, b, preferred_element_type=F32)


def window_of(row, col):
    return (
        pl.multiple_of(row // SUBLANES * SUBLANES, SUBLANES),
        pl.multiple_of(col // LANES * LANES, LANES),
        row % SUBLANES,
        col % LANES,
    )


def cut(wide, down, right, length):
    wide = pltpu.roll(wide, 2 * LANES - right, 1)[:, :length]
    return pltpu.roll(wide, length + SUBLANES - down, 0)[:length]


def placed_in(term, down, right):
    tall = jnp.concatenate([term, jnp.zeros((SUBLANES, term.shape[1]), F32)], axis=0)
    tall = pltpu.roll(pltpu.roll(tall, down, 0), right, 1)
    first = lax.broadcasted_iota(jnp.int32, tall.shape, 1) >= right
    return jnp.concatenate([jnp.where(first, tall, 0.0), jnp.where(first, 0.0, tall)], axis=1)


def patches_kernel(place, first, second, third, patch, density, extended):
    slots, _, length, _ = patch.shape
    rows = first.shape[1]
    for step, tile in enumerate((first, second, third)):
        extended[:, step * rows : (step + 1) * rows] = tile[...]
    total = None
    for slot in range(slots):
        row, col, used = place[3 * slot], place[3 * slot + 1], place[3 * slot + 2]
        top, left, down, right = window_of(row, col)
        here = 0.0
        for part in range(2):
            wide = extended[part, pl.ds(top, length + SUBLANES), pl.ds(left, 2 * LANES)]
            window = cut(wide, down, right, length)
            patch[slot, part] = window
            here = here + window * window
        here = here * used.astype(F32)
        total = here if total is None else total + here
    density[...] = total


def whole_probe(probes, k, part, parity):
    return jnp.concatenate([probes[k, parity, part], probes[k, 1 - parity, part]], axis=0)


def wave_kernel(place, me, patch, density, probes, amplitude, table, windows, *rest):
    (kept, sent, *terms), (sums, x_hi, x_lo, y_hi, y_lo, far, own_probe) = rest[:-7], rest[-7:]
    slots, _, length, _ = patch.shape
    modes = probes.shape[0]
    half = length // 2
    scan = me[0]
    parity = scan % 2

    def from_left(which):
        for pair in range(modes // 2):
            cols = slice(2 * pair * length, 2 * (pair + 1) * length)
            hi, lo = x_hi[:, cols], x_lo[:, cols]
            out = dot(table[which, 0], hi) + dot(table[which, 0], lo) + dot(table[which, 1], hi)
            hi, lo = split(out)
            for k in range(2):
                rows = slice((2 * pair + k) * length, (2 * pair + k + 1) * length)
                cols = slice(k * length, (k + 1) * length)
                y_hi[rows, :length], y_hi[rows, length:] = hi[:length, cols], hi[length:, cols]
                y_lo[rows, :length], y_lo[rows, length:] = lo[:length, cols], lo[length:, cols]

    def from_right(which, k):
        rows = slice(k * length, (k + 1) * length)
        hi, lo = y_hi[rows], y_lo[rows]
        return dot(hi, table[which, 0]) + dot(lo, table[which, 0]) + dot(hi, table[which, 1])

    def set_columns(k, real, imag):
        cols = slice(k * length, (k + 1) * length)
        hi, lo = split(real)
        x_hi[:length, cols], x_lo[:length, cols] = hi, lo
        hi, lo = split(imag)
        x_hi[length:, cols], x_lo[length:, cols] = hi, lo

    sums[...] = jnp.zeros_like(sums)
    for k in range(modes):
        for part in range(2):
            own_probe[k, part] = whole_probe(probes, k, part, parity)
    for slot in range(slots):
        row, col, used = place[3 * slot], place[3 * slot + 1], place[3 * slot + 2].astype(F32)
        obj_re, obj_im = patch[slot, 0], patch[slot, 1]
        for k in range(modes):
            pr, pi = own_probe[k, 0], own_probe[k, 1]
            set_columns(k, pr * obj_re - pi * obj_im, pr * obj_im + pi * obj_re)
        from_left(0)
        intensity = 0.0
        for k in range(modes):
            wave = from_right(1, k)
            far[k] = wave
            square = wave * wave
            intensity = intensity + square[:, :length] + square[:, length:]
        factor = amplitude[slot] / jnp.sqrt(jnp.maximum(intensity, 1.0))
        for k in range(modes):
            set_columns(k, far[k, :, :length] * factor, far[k, :, length:] * factor)
        from_left(1)
        num_re, num_im = 0.0, 0.0
        for k in range(modes):
            near = from_right(0, k)
            pr, pi = own_probe[k, 0], own_probe[k, 1]
            change_re = (near[:, :length] - (pr * obj_re - pi * obj_im)) * used
            change_im = (near[:, length:] - (pr * obj_im + pi * obj_re)) * used
            num_re = num_re + (pr * change_re + pi * change_im)
            num_im = num_im + (pr * change_im - pi * change_re)
            grad_re = obj_re * change_re + obj_im * change_im
            grad_im = obj_re * change_im - obj_im * change_re
            out, at = (kept, k) if k < modes // 2 else (sent, k - modes // 2)
            for part, grad in enumerate((grad_re, grad_im)):
                for top in range(2):
                    where = (at, parity ^ top, slice(part * half, (part + 1) * half))
                    piece = grad[top * half : (top + 1) * half]
                    out[where] = piece if slot == 0 else out[where] + piece
        top, left, down, right = window_of(row, col)
        for part, term in enumerate((num_re, num_im)):
            sums[part, pl.ds(top, length + SUBLANES), pl.ds(left, 2 * LANES)] += placed_in(term, down, right)
    for out in (kept, sent):
        for at in range(modes // 2):
            for top in range(2):
                out[at, parity ^ top, 2 * half :] = density[top * half : (top + 1) * half]
    data_rows = terms[0].shape[0] - windows.shape[0]
    tile_rows = data_rows // 2
    for step, out in enumerate(terms):
        for part in range(2):
            out[part * tile_rows : (part + 1) * tile_rows] = sums[part, step * tile_rows : (step + 1) * tile_rows]
        out[data_rows:] = jnp.zeros((windows.shape[0], out.shape[1]), F32)
        out[data_rows:, LANES : 2 * LANES] = windows[...]


def weight_of(table, me, probes, grid, scan_steps, mode_steps, rows, cols, tile_rows, band_cols, acc):
    modes, length = probes.shape[0], probes.shape[-1]
    above, left = (acc.shape[0] - rows - length, acc.shape[1] - cols - length)
    scan, mode = me[0], me[1]
    power = 0.0
    for k in range(modes):
        real, imag = (whole_probe(probes, k, part, scan % 2) for part in range(2))
        power = power + (real * real + imag * imag)
    acc[...] = jnp.zeros_like(acc)
    for ds in scan_steps:
        for dm in mode_steps:
            inside = (scan + ds >= 0) & (scan + ds < grid[0]) & (mode + dm >= 0) & (mode + dm < grid[1])
            first = jnp.where(inside, (scan + ds) * grid[1] + mode + dm, 0) * TABLE
            for slot in range(TABLE // 3):
                row = table[first + 3 * slot] - scan * tile_rows
                col = table[first + 3 * slot + 1] - mode * band_cols
                used = inside & (table[first + 3 * slot + 2] > 0)
                used &= (row > -length) & (row < rows) & (col > -length) & (col < cols)

                @pl.when(used)
                def _():
                    top, before, down, right = window_of(row + above, col + left)
                    acc[pl.ds(top, length + SUBLANES), pl.ds(before, 2 * LANES)] += placed_in(power, down, right)

    return acc[pl.ds(above, rows), pl.ds(left, cols)] + 1.0


def join_kernel(band_cols, me, inner, outer, entries, from_a, from_b, new_inner, new_outer, for_a, for_b):
    data_rows = inner.shape[0]
    rim = for_a.shape[1]
    lower = (me[0] // 2 % 2 == 0).astype(F32)
    even = (me[1] % 2 == 0).astype(F32)
    a, b = from_a[:data_rows], from_b[:data_rows]
    tiles = (inner[...] + b * lower + a * (1.0 - lower), outer[...] + a * lower + b * (1.0 - lower))
    new_inner[...], new_outer[...] = tiles
    for at, tile in enumerate(tiles):
        rows = slice(at * data_rows, (at + 1) * data_rows)
        left, right = tile[:, :rim], tile[:, band_cols:]
        for_a[rows] = right * even + left * (1.0 - even)
        for_b[rows] = left * even + right * (1.0 - even)
    rest = entries[...] + from_a[data_rows:, LANES : 2 * LANES] + from_b[data_rows:, LANES : 2 * LANES]
    for_a[2 * data_rows :] = rest
    for_b[2 * data_rows :] = rest


def inner_kernel(grid, band_cols, table, me, first, third, probes, inner, outer, from_a, from_b, new_first, new_third, passed, acc):
    _, tile_rows, cols = first.shape
    rim = from_a.shape[1]
    scan, mode = me[0], me[1]
    weight = weight_of(
        table, me, probes, grid, range(-2, 3), range(-1, 2), 3 * tile_rows, cols, tile_rows, band_cols, acc
    )
    inside = jnp.where(lax.broadcasted_iota(jnp.int32, (tile_rows, cols), 1) < (grid[1] - mode) * band_cols, 1.0, 0.0)
    beyond = inside * (scan + 2 < grid[0]).astype(F32)
    is_first = (scan % 2).astype(F32)
    even = (mode % 2 == 0).astype(F32)
    for part in range(2):
        updated = []
        for at, (term, tile, keep) in enumerate(((inner, first, inside), (outer, third, beyond))):
            a, b = (ref[slice((2 * at + part) * tile_rows, (2 * at + part + 1) * tile_rows)] for ref in (from_a, from_b))
            left, right = b * even + a * (1.0 - even), a * even + b * (1.0 - even)
            term = term[part * tile_rows : (part + 1) * tile_rows]
            term = jnp.concatenate([term[:, :rim] + left, term[:, rim:band_cols], term[:, band_cols:] + right], axis=1)
            updated.append(tile[part] + keep * term / weight[2 * at * tile_rows : (2 * at + 1) * tile_rows])
        new_first[part], new_third[part] = updated
        passed[part] = updated[0] * is_first + updated[1] * (1.0 - is_first)


def last_kernel(grid, table, me, probes, weight, acc):
    rows, cols = weight.shape
    weight[...] = weight_of(table, me, probes, grid, range(-2, 1), range(-1, 1), rows, cols, rows, cols, acc)


VMEM = pl.BlockSpec(memory_space=pltpu.VMEM)
SMEM = pl.BlockSpec(memory_space=pltpu.SMEM)


def call(kernel, out_shape, in_specs, scratch=(), flops=0, moved=0):
    return pl.pallas_call(
        kernel,
        out_shape=out_shape,
        in_specs=in_specs,
        out_specs=jax.tree.map(lambda _: VMEM, out_shape),
        scratch_shapes=list(scratch),
        compiler_params=pltpu.CompilerParams(vmem_limit_bytes=16 * 2**20),
        cost_estimate=pl.CostEstimate(flops=flops, bytes_accessed=moved, transcendentals=0),
    )


def local(object_field, probe, amplitude, offsets, counts):
    tile_rows, band_cols = object_field.shape[1:]
    scans, modes = lax.axis_size("scan"), lax.axis_size("mode")
    scan, mode = lax.axis_index("scan"), lax.axis_index("mode")
    length = probe.shape[2]
    slots = amplitude.shape[0]
    reach = -(-length // tile_rows)
    ext_rows, ext_cols = tile_rows + length, band_cols + length
    table = jnp.asarray(fresnel_parts(length))
    used = (jnp.arange(slots, dtype=jnp.int32) < counts[0]).astype(jnp.int32)
    corner = jnp.stack([scan * tile_rows, mode * band_cols]).astype(jnp.int32)
    place = jnp.concatenate([offsets - corner, used[:, None]], axis=1).reshape(-1)

    me = jnp.stack([scan, mode]).astype(jnp.int32)
    parity = scan % 2
    near, far = bits_of("mode")
    half = length // 2

    entry = jnp.concatenate([offsets, used[:, None]], axis=1).reshape(-1)
    entry = jnp.pad(entry, (0, TABLE - entry.shape[0])).astype(F32)
    table_rows = -(-scans * modes * TABLE // (SUBLANES * LANES)) * SUBLANES
    blocks = jnp.arange(table_rows * LANES // TABLE)
    windows = jnp.where((blocks == scan * modes + mode)[:, None], entry[None, :], 0.0).reshape(-1, LANES)
    data_rows = 2 * tile_rows
    even, odd = (parity == 0).astype(F32), (parity == 1).astype(F32)
    even_mode = (mode % 2 == 0).astype(F32)
    lower = (scan // 2 % 2 == 0).astype(F32)

    def sds(*shape):
        return jax.ShapeDtypeStruct(shape, F32)

    def as_halves(value):
        value = value.reshape(value.shape[0], 2, 2, half, length).swapaxes(1, 2)
        return jnp.where(parity == 0, value, value[:, ::-1])

    def scratch(rows, cols):
        return [pltpu.VMEM((reach * tile_rows + rows + length, band_cols + cols + length), F32)]

    def joined_rows(terms):
        arrived = swapped(terms[1], "scan", 1)
        inner = terms[0][:data_rows] + arrived[:data_rows] * odd
        outer = terms[2][:data_rows] + arrived[:data_rows] * even
        entries = terms[0][data_rows:] + arrived[data_rows:]
        a = paired(jnp.concatenate([outer * lower + inner * (1.0 - lower), entries]), "scan", 2, 0)
        b = paired(jnp.concatenate([inner * lower + outer * (1.0 - lower), entries]), "scan", 2, 1)
        rows = 2 * data_rows + table_rows
        return call(
            functools.partial(join_kernel, band_cols),
            [sds(data_rows, ext_cols)] * 2 + [sds(rows, length)] * 2,
            [SMEM] + [VMEM] * 5,
            flops=2**20,
            moved=2**20,
        )(me, inner, outer, entries[:, LANES : 2 * LANES], a, b)

    def inner_update(first, third, probes, inner, outer, for_a, for_b):
        a, b = paired(for_a, "mode", 1, 0), paired(for_b, "mode", 1, 1)
        entries = (for_a + a + b)[2 * data_rows :].astype(jnp.int32).reshape(-1)
        first, third, passed = call(
            functools.partial(inner_kernel, (scans, modes), band_cols),
            [sds(2, tile_rows, ext_cols)] * 3,
            [SMEM, SMEM] + [VMEM] * 7,
            scratch(3 * tile_rows, ext_cols),
            flops=2**20,
            moved=2**20,
        )(entries, me, first, third, probes, inner, outer, a, b)
        return first, third, passed, entries

    def last_update(tile, probes, terms, entries):
        arrived = swapped(terms[1][:data_rows], "scan", 1)
        third = terms[2][:data_rows] + arrived * even
        first = terms[0][:data_rows] + arrived * odd + shifted(third, "scan", 2)
        return first

    def last_part(tile, probes, first, entries):
        weight = call(
            functools.partial(last_kernel, (scans, modes)),
            sds(tile_rows, band_cols),
            [SMEM, SMEM, VMEM],
            scratch(tile_rows, band_cols),
            flops=2**20,
            moved=2**20,
        )(entries, me, probes)
        margin = shifted(first[:, band_cols:], "mode", 1)
        terms = jnp.concatenate([first[:, :length] + margin, first[:, length:band_cols]], axis=1)
        return tile[:, :, :band_cols] + terms.reshape(2, tile_rows, band_cols) / weight

    probes = as_halves(probe)
    probes = jnp.concatenate([probes, swapped(probes, "mode", far)], axis=0)
    tiles = [object_field, shifted(object_field, "scan", -1), shifted(object_field, "scan", -2)]
    tiles = jnp.concatenate(tiles, axis=1)
    tiles = jnp.concatenate([tiles, shifted(tiles[:, :, :length], "mode", -1)], axis=2)
    probes = after(probes, tiles)
    probes = jnp.concatenate([probes, swapped(probes, "mode", near)], axis=0)
    first, second, third = (tiles[:, step * tile_rows : (step + 1) * tile_rows] for step in range(3))
    for iteration in range(ITERS):
        last = iteration == ITERS - 1
        patch, density = call(
            patches_kernel,
            (sds(slots, 2, length, length), sds(length, length)),
            [SMEM] + [VMEM] * 3,
            [pltpu.VMEM((2, ext_rows, ext_cols), F32)],
            flops=2**20,
            moved=2**20,
        )(place, first, second, third)
        rows_out = data_rows + table_rows
        kept, sent, *terms = call(
            wave_kernel,
            (*[sds(modes // 2, 2, 3 * half, length)] * 2, *[sds(rows_out, ext_cols)] * 3),
            [SMEM, SMEM] + [VMEM] * 6,
            [pltpu.VMEM((2, ext_rows, ext_cols), F32)]
            + [pltpu.VMEM((2 * length, modes * length), BF16)] * 2
            + [pltpu.VMEM((modes * length, 2 * length), BF16)] * 2
            + [pltpu.VMEM((modes, length, 2 * length), F32), pltpu.VMEM((modes, 2, length, length), F32)],
            flops=slots * modes * 4 * 3 * 2 * 4 * length**3,
            moved=4 * 2**20,
        )(place, me, patch, density, probes, amplitude, table, windows)
        kept = kept + swapped(sent, "mode", near)
        if last:
            kept, terms = lax.optimization_barrier((kept, terms))
        pass
        own = kept[0, 0] + across(kept[0, 1], 1, 0) + across(kept[1, 0], 0, far) + across(kept[1, 1], 1, far)
        if not last:
            joined = joined_rows(terms)
        pass
        for bit in bits_of("scan")[1:][:: -1 if last else 1]:
            own = own + swapped(own, "scan", bit)
            pass
        if not last:
            first, third, passed, entries = inner_update(first, third, probes, *joined)
        else:
            inner = last_update(first, probes, terms[:3], entries)
            own = after(own, inner)
        probe = probes[0, 0] + own[: 2 * half].reshape(2, half, length) / (own[2 * half :] + 1.0)
        if not last:
            second = swapped(passed, "scan", 1)
            probes = jnp.stack(
                [
                    jnp.stack([probe, across(probe, 1, 0)]),
                    jnp.stack([across(probe, 0, far), across(probe, 1, far)]),
                ]
            )
            probes = after(probes, second)
            probes = jnp.concatenate([probes, swapped(probes, "mode", near)], axis=0)
        else:
            object_field = last_part(first, probes, inner, entries)
            probe = jnp.stack([probe, across(probe, 1, 0)])
            probe = jnp.where(parity == 0, probe, probe[::-1]).swapaxes(0, 1).reshape(1, 2, length, length)
    return (object_field, probe)


def solution(mesh):
    placed = (
        P(None, "scan", "mode"),
        P("mode", None, None, None),
        P(("scan", "mode"), None, None),
        P(("scan", "mode"), None),
        P(("scan", "mode")),
    )
    return jax.shard_map(
        local,
        mesh=mesh,
        in_specs=placed,
        out_specs=(P(None, "scan", "mode"), P("mode", None, None, None)),
        check_vma=False,
    )
```

```python
import functools
import math

import jax
import jax.numpy as jnp
import numpy as np
from jax import lax
from jax.experimental import pallas as pl
from jax.experimental.pallas import tpu as pltpu
from jax.sharding import PartitionSpec as P

ITERS = 2
SUBLANES, LANES = 8, 128
F32 = jnp.float32
BF16 = jnp.bfloat16
TABLE = 8


def shifted(value, axis, steps):
    count = lax.axis_size(axis)
    initial, last = (max(0, -steps), min(count, count - steps))
    return lax.ppermute(value, axis, [(source, source + steps) for source in range(initial, last)])


def swapped(value, axis, bit):
    return lax.ppermute(value, axis, [(i, i ^ bit) for i in range(lax.axis_size(axis))])


def paired(value, axis, step, phase):
    lower = [i for i in range(lax.axis_size(axis) - step) if i // step % 2 == phase]
    return lax.ppermute(value, axis, [(i, i + step) for i in lower] + [(i + step, i) for i in lower])


def across(value, scan_bit, mode_bit):
    scans, modes = lax.axis_size("scan"), lax.axis_size("mode")
    other = scan_bit * modes + mode_bit
    return lax.ppermute(value, ("scan", "mode"), [(i, i ^ other) for i in range(scans * modes)])


def after(value, others):
    return lax.optimization_barrier((value, others))[0]


def bits_of(axis):
    return [1 << b for b in range(lax.axis_size(axis).bit_length() - 1)]


def gathered(value, axis):
    for bit in reversed(bits_of(axis)):
        value = jnp.concatenate([value, swapped(value, axis, bit)], axis=0)
    return value


@functools.lru_cache
def fresnel_parts(length):
    ids = np.arange(length, dtype=np.int64)
    phase = ids[:, None] * ids[None, :] % length
    centred = ids - length // 2
    chirp = centred * centred % (4 * length)
    angle = -2.0 * math.pi / length * phase + math.pi / (2 * length) * chirp[None, :]
    real, imag = np.cos(angle) / math.sqrt(length), np.sin(angle) / math.sqrt(length)
    whole = np.block([[real, -imag], [imag, real]])
    parts = []
    for matrix in (whole, whole.T):
        high = matrix.astype(jnp.bfloat16)
        low = (matrix - high.astype(np.float64)).astype(jnp.bfloat16)
        parts.append(np.stack([high, low]))
    return np.stack(parts)


def split(value):
    high = value.astype(BF16)
    return high, (value - high.astype(F32)).astype(BF16)


def dot(a, b):
    return jnp.dot(a, b, preferred_element_type=F32)


def window_of(row, col):
    return (
        pl.multiple_of(row // SUBLANES * SUBLANES, SUBLANES),
        pl.multiple_of(col // LANES * LANES, LANES),
        row % SUBLANES,
        col % LANES,
    )


def cut(wide, down, right, length):
    wide = pltpu.roll(wide, 2 * LANES - right, 1)[:, :length]
    return pltpu.roll(wide, length + SUBLANES - down, 0)[:length]


def placed_in(term, down, right):
    tall = jnp.concatenate([term, jnp.zeros((SUBLANES, term.shape[1]), F32)], axis=0)
    tall = pltpu.roll(pltpu.roll(tall, down, 0), right, 1)
    first = lax.broadcasted_iota(jnp.int32, tall.shape, 1) >= right
    return jnp.concatenate([jnp.where(first, tall, 0.0), jnp.where(first, 0.0, tall)], axis=1)


def patches_kernel(place, first, second, third, patch, density, extended):
    slots, _, length, _ = patch.shape
    rows = first.shape[1]
    for step, tile in enumerate((first, second, third)):
        extended[:, step * rows : (step + 1) * rows] = tile[...]
    total = None
    for slot in range(slots):
        row, col, used = place[3 * slot], place[3 * slot + 1], place[3 * slot + 2]
        top, left, down, right = window_of(row, col)
        here = 0.0
        for part in range(2):
            wide = extended[part, pl.ds(top, length + SUBLANES), pl.ds(left, 2 * LANES)]
            window = cut(wide, down, right, length)
            patch[slot, part] = window
            here = here + window * window
        here = here * used.astype(F32)
        total = here if total is None else total + here
    density[...] = total


def whole_probe(probes, k, part, parity):
    return jnp.concatenate([probes[k, parity, part], probes[k, 1 - parity, part]], axis=0)


def wave_kernel(place, me, patch, density, probes, amplitude, table, windows, *rest):
    (kept, sent, *terms), (sums, x_hi, x_lo, y_hi, y_lo, far, own_probe) = rest[:-7], rest[-7:]
    slots, _, length, _ = patch.shape
    modes = probes.shape[0]
    half = length // 2
    scan = me[0]
    parity = scan % 2

    def from_left(which):
        for pair in range(modes // 2):
            cols = slice(2 * pair * length, 2 * (pair + 1) * length)
            hi, lo = x_hi[:, cols], x_lo[:, cols]
            out = dot(table[which, 0], hi) + dot(table[which, 0], lo) + dot(table[which, 1], hi)
            hi, lo = split(out)
            for k in range(2):
                rows = slice((2 * pair + k) * length, (2 * pair + k + 1) * length)
                cols = slice(k * length, (k + 1) * length)
                y_hi[rows, :length], y_hi[rows, length:] = hi[:length, cols], hi[length:, cols]
                y_lo[rows, :length], y_lo[rows, length:] = lo[:length, cols], lo[length:, cols]

    def from_right(which, k):
        rows = slice(k * length, (k + 1) * length)
        hi, lo = y_hi[rows], y_lo[rows]
        return dot(hi, table[which, 0]) + dot(lo, table[which, 0]) + dot(hi, table[which, 1])

    def set_columns(k, real, imag):
        cols = slice(k * length, (k + 1) * length)
        hi, lo = split(real)
        x_hi[:length, cols], x_lo[:length, cols] = hi, lo
        hi, lo = split(imag)
        x_hi[length:, cols], x_lo[length:, cols] = hi, lo

    sums[...] = jnp.zeros_like(sums)
    for k in range(modes):
        for part in range(2):
            own_probe[k, part] = whole_probe(probes, k, part, parity)
    for slot in range(slots):
        row, col, used = place[3 * slot], place[3 * slot + 1], place[3 * slot + 2].astype(F32)
        obj_re, obj_im = patch[slot, 0], patch[slot, 1]
        for k in range(modes):
            pr, pi = own_probe[k, 0], own_probe[k, 1]
            set_columns(k, pr * obj_re - pi * obj_im, pr * obj_im + pi * obj_re)
        from_left(0)
        intensity = 0.0
        for k in range(modes):
            wave = from_right(1, k)
            far[k] = wave
            square = wave * wave
            intensity = intensity + square[:, :length] + square[:, length:]
        factor = amplitude[slot] / jnp.sqrt(jnp.maximum(intensity, 1.0))
        for k in range(modes):
            set_columns(k, far[k, :, :length] * factor, far[k, :, length:] * factor)
        from_left(1)
        num_re, num_im = 0.0, 0.0
        for k in range(modes):
            near = from_right(0, k)
            pr, pi = own_probe[k, 0], own_probe[k, 1]
            change_re = (near[:, :length] - (pr * obj_re - pi * obj_im)) * used
            change_im = (near[:, length:] - (pr * obj_im + pi * obj_re)) * used
            num_re = num_re + (pr * change_re + pi * change_im)
            num_im = num_im + (pr * change_im - pi * change_re)
            grad_re = obj_re * change_re + obj_im * change_im
            grad_im = obj_re * change_im - obj_im * change_re
            out, at = (kept, k) if k < modes // 2 else (sent, k - modes // 2)
            for part, grad in enumerate((grad_re, grad_im)):
                for top in range(2):
                    where = (at, parity ^ top, slice(part * half, (part + 1) * half))
                    piece = grad[top * half : (top + 1) * half]
                    out[where] = piece if slot == 0 else out[where] + piece
        top, left, down, right = window_of(row, col)
        for part, term in enumerate((num_re, num_im)):
            sums[part, pl.ds(top, length + SUBLANES), pl.ds(left, 2 * LANES)] += placed_in(term, down, right)
    for out in (kept, sent):
        for at in range(modes // 2):
            for top in range(2):
                out[at, parity ^ top, 2 * half :] = density[top * half : (top + 1) * half]
    data_rows = terms[0].shape[0] - windows.shape[0]
    tile_rows = data_rows // 2
    for step, out in enumerate(terms):
        for part in range(2):
            out[part * tile_rows : (part + 1) * tile_rows] = sums[part, step * tile_rows : (step + 1) * tile_rows]
        out[data_rows:] = jnp.zeros((windows.shape[0], out.shape[1]), F32)
        out[data_rows:, LANES : 2 * LANES] = windows[...]


def weight_of(table, me, probes, grid, scan_steps, mode_steps, rows, cols, tile_rows, band_cols, acc):
    modes, length = probes.shape[0], probes.shape[-1]
    above, left = (acc.shape[0] - rows - length, acc.shape[1] - cols - length)
    scan, mode = me[0], me[1]
    power = 0.0
    for k in range(modes):
        real, imag = (whole_probe(probes, k, part, scan % 2) for part in range(2))
        power = power + (real * real + imag * imag)
    acc[...] = jnp.zeros_like(acc)
    for ds in scan_steps:
        for dm in mode_steps:
            inside = (scan + ds >= 0) & (scan + ds < grid[0]) & (mode + dm >= 0) & (mode + dm < grid[1])
            first = jnp.where(inside, (scan + ds) * grid[1] + mode + dm, 0) * TABLE
            for slot in range(TABLE // 3):
                row = table[first + 3 * slot] - scan * tile_rows
                col = table[first + 3 * slot + 1] - mode * band_cols
                used = inside & (table[first + 3 * slot + 2] > 0)
                used &= (row > -length) & (row < rows) & (col > -length) & (col < cols)

                @pl.when(used)
                def _():
                    top, before, down, right = window_of(row + above, col + left)
                    acc[pl.ds(top, length + SUBLANES), pl.ds(before, 2 * LANES)] += placed_in(power, down, right)

    return acc[pl.ds(above, rows), pl.ds(left, cols)] + 1.0


def join_kernel(band_cols, me, inner, outer, entries, from_a, from_b, new_inner, new_outer, for_a, for_b):
    data_rows = inner.shape[0]
    rim = for_a.shape[1]
    lower = (me[0] // 2 % 2 == 0).astype(F32)
    even = (me[1] % 2 == 0).astype(F32)
    a, b = from_a[:data_rows], from_b[:data_rows]
    tiles = (inner[...] + b * lower + a * (1.0 - lower), outer[...] + a * lower + b * (1.0 - lower))
    new_inner[...], new_outer[...] = tiles
    for at, tile in enumerate(tiles):
        rows = slice(at * data_rows, (at + 1) * data_rows)
        left, right = tile[:, :rim], tile[:, band_cols:]
        for_a[rows] = right * even + left * (1.0 - even)
        for_b[rows] = left * even + right * (1.0 - even)
    rest = entries[...] + from_a[data_rows:, LANES : 2 * LANES] + from_b[data_rows:, LANES : 2 * LANES]
    for_a[2 * data_rows :] = rest
    for_b[2 * data_rows :] = rest


def inner_kernel(grid, band_cols, table, me, first, third, probes, inner, outer, from_a, from_b, new_first, new_third, passed, acc):
    _, tile_rows, cols = first.shape
    rim = from_a.shape[1]
    scan, mode = me[0], me[1]
    weight = weight_of(
        table, me, probes, grid, range(-2, 3), range(-1, 2), 3 * tile_rows, cols, tile_rows, band_cols, acc
    )
    inside = jnp.where(lax.broadcasted_iota(jnp.int32, (tile_rows, cols), 1) < (grid[1] - mode) * band_cols, 1.0, 0.0)
    beyond = inside * (scan + 2 < grid[0]).astype(F32)
    is_first = (scan % 2).astype(F32)
    even = (mode % 2 == 0).astype(F32)
    for part in range(2):
        updated = []
        for at, (term, tile, keep) in enumerate(((inner, first, inside), (outer, third, beyond))):
            a, b = (ref[slice((2 * at + part) * tile_rows, (2 * at + part + 1) * tile_rows)] for ref in (from_a, from_b))
            left, right = b * even + a * (1.0 - even), a * even + b * (1.0 - even)
            term = term[part * tile_rows : (part + 1) * tile_rows]
            term = jnp.concatenate([term[:, :rim] + left, term[:, rim:band_cols], term[:, band_cols:] + right], axis=1)
            updated.append(tile[part] + keep * term / weight[2 * at * tile_rows : (2 * at + 1) * tile_rows])
        new_first[part], new_third[part] = updated
        passed[part] = updated[0] * is_first + updated[1] * (1.0 - is_first)


def last_kernel(grid, table, me, probes, weight, acc):
    rows, cols = weight.shape
    weight[...] = weight_of(table, me, probes, grid, range(-2, 1), range(-1, 1), rows, cols, rows, cols, acc)


VMEM = pl.BlockSpec(memory_space=pltpu.VMEM)
SMEM = pl.BlockSpec(memory_space=pltpu.SMEM)


def call(kernel, out_shape, in_specs, scratch=(), flops=0, moved=0):
    return pl.pallas_call(
        kernel,
        out_shape=out_shape,
        in_specs=in_specs,
        out_specs=jax.tree.map(lambda _: VMEM, out_shape),
        scratch_shapes=list(scratch),
        compiler_params=pltpu.CompilerParams(vmem_limit_bytes=16 * 2**20),
        cost_estimate=pl.CostEstimate(flops=flops, bytes_accessed=moved, transcendentals=0),
    )


def local(object_field, probe, amplitude, offsets, counts):
    tile_rows, band_cols = object_field.shape[1:]
    scans, modes = lax.axis_size("scan"), lax.axis_size("mode")
    scan, mode = lax.axis_index("scan"), lax.axis_index("mode")
    length = probe.shape[2]
    slots = amplitude.shape[0]
    reach = -(-length // tile_rows)
    ext_rows, ext_cols = tile_rows + length, band_cols + length
    table = jnp.asarray(fresnel_parts(length))
    used = (jnp.arange(slots, dtype=jnp.int32) < counts[0]).astype(jnp.int32)
    corner = jnp.stack([scan * tile_rows, mode * band_cols]).astype(jnp.int32)
    place = jnp.concatenate([offsets - corner, used[:, None]], axis=1).reshape(-1)

    me = jnp.stack([scan, mode]).astype(jnp.int32)
    parity = scan % 2
    near, far = bits_of("mode")
    half = length // 2

    entry = jnp.concatenate([offsets, used[:, None]], axis=1).reshape(-1)
    entry = jnp.pad(entry, (0, TABLE - entry.shape[0])).astype(F32)
    table_rows = -(-scans * modes * TABLE // (SUBLANES * LANES)) * SUBLANES
    blocks = jnp.arange(table_rows * LANES // TABLE)
    windows = jnp.where((blocks == scan * modes + mode)[:, None], entry[None, :], 0.0).reshape(-1, LANES)
    data_rows = 2 * tile_rows
    even, odd = (parity == 0).astype(F32), (parity == 1).astype(F32)
    even_mode = (mode % 2 == 0).astype(F32)
    lower = (scan // 2 % 2 == 0).astype(F32)

    def sds(*shape):
        return jax.ShapeDtypeStruct(shape, F32)

    def as_halves(value):
        value = value.reshape(value.shape[0], 2, 2, half, length).swapaxes(1, 2)
        return jnp.where(parity == 0, value, value[:, ::-1])

    def scratch(rows, cols):
        return [pltpu.VMEM((reach * tile_rows + rows + length, band_cols + cols + length), F32)]

    def joined_rows(terms):
        arrived = swapped(terms[1], "scan", 1)
        inner = terms[0][:data_rows] + arrived[:data_rows] * odd
        outer = terms[2][:data_rows] + arrived[:data_rows] * even
        entries = terms[0][data_rows:] + arrived[data_rows:]
        a = paired(jnp.concatenate([outer * lower + inner * (1.0 - lower), entries]), "scan", 2, 0)
        b = paired(jnp.concatenate([inner * lower + outer * (1.0 - lower), entries]), "scan", 2, 1)
        rows = 2 * data_rows + table_rows
        return call(
            functools.partial(join_kernel, band_cols),
            [sds(data_rows, ext_cols)] * 2 + [sds(rows, length)] * 2,
            [SMEM] + [VMEM] * 5,
            flops=2**20,
            moved=2**20,
        )(me, inner, outer, entries[:, LANES : 2 * LANES], a, b)

    def inner_update(first, third, probes, inner, outer, for_a, for_b):
        a, b = paired(for_a, "mode", 1, 0), paired(for_b, "mode", 1, 1)
        entries = (for_a + a + b)[2 * data_rows :].astype(jnp.int32).reshape(-1)
        first, third, passed = call(
            functools.partial(inner_kernel, (scans, modes), band_cols),
            [sds(2, tile_rows, ext_cols)] * 3,
            [SMEM, SMEM] + [VMEM] * 7,
            scratch(3 * tile_rows, ext_cols),
            flops=2**20,
            moved=2**20,
        )(entries, me, first, third, probes, inner, outer, a, b)
        return first, third, passed, entries

    def with_margin(term, margin):
        return jnp.concatenate([term[:, :length] + margin, term[:, length:band_cols]], axis=1)

    def last_update(terms):
        terms = [term[:data_rows] for term in terms]
        margin = shifted(jnp.concatenate([term[:, band_cols:] for term in terms]), "mode", 1)
        terms = [with_margin(term, margin[i * data_rows : (i + 1) * data_rows]) for i, term in enumerate(terms)]
        arrived = swapped(terms[1], "scan", 1)
        return terms[0] + arrived * odd, terms[2] + arrived * even

    def last_part(tile, probes, terms, entries):
        weight = call(
            functools.partial(last_kernel, (scans, modes)),
            sds(tile_rows, band_cols),
            [SMEM, SMEM, VMEM],
            scratch(tile_rows, band_cols),
            flops=2**20,
            moved=2**20,
        )(entries, me, probes)
        return tile[:, :, :band_cols] + terms.reshape(2, tile_rows, band_cols) / weight

    probes = as_halves(probe)
    probes = jnp.concatenate([probes, swapped(probes, "mode", far)], axis=0)
    tiles = [object_field, shifted(object_field, "scan", -1), shifted(object_field, "scan", -2)]
    tiles = jnp.concatenate(tiles, axis=1)
    tiles = jnp.concatenate([tiles, shifted(tiles[:, :, :length], "mode", -1)], axis=2)
    probes = after(probes, tiles)
    probes = jnp.concatenate([probes, swapped(probes, "mode", near)], axis=0)
    first, second, third = (tiles[:, step * tile_rows : (step + 1) * tile_rows] for step in range(3))
    for iteration in range(ITERS):
        last = iteration == ITERS - 1
        patch, density = call(
            patches_kernel,
            (sds(slots, 2, length, length), sds(length, length)),
            [SMEM] + [VMEM] * 3,
            [pltpu.VMEM((2, ext_rows, ext_cols), F32)],
            flops=2**20,
            moved=2**20,
        )(place, first, second, third)
        rows_out = data_rows + table_rows
        kept, sent, *terms = call(
            wave_kernel,
            (*[sds(modes // 2, 2, 3 * half, length)] * 2, *[sds(rows_out, ext_cols)] * 3),
            [SMEM, SMEM] + [VMEM] * 6,
            [pltpu.VMEM((2, ext_rows, ext_cols), F32)]
            + [pltpu.VMEM((2 * length, modes * length), BF16)] * 2
            + [pltpu.VMEM((modes * length, 2 * length), BF16)] * 2
            + [pltpu.VMEM((modes, length, 2 * length), F32), pltpu.VMEM((modes, 2, length, length), F32)],
            flops=slots * modes * 4 * 3 * 2 * 4 * length**3,
            moved=4 * 2**20,
        )(place, me, patch, density, probes, amplitude, table, windows)
        kept = kept + swapped(sent, "mode", near)
        if last:
            kept, terms = lax.optimization_barrier((kept, terms))
        pass
        own = kept[0, 0] + across(kept[0, 1], 1, 0) + across(kept[1, 0], 0, far) + across(kept[1, 1], 1, far)
        if not last:
            joined = joined_rows(terms)
        pass
        for bit in bits_of("scan")[1:]:
            own = own + swapped(own, "scan", bit)
            pass
        if not last:
            first, third, passed, entries = inner_update(first, third, probes, *joined)
        else:
            inner, outer = last_update(terms)
            inner = inner + shifted(outer, "scan", 2)
        probe = probes[0, 0] + own[: 2 * half].reshape(2, half, length) / (own[2 * half :] + 1.0)
        if not last:
            second = swapped(passed, "scan", 1)
            probes = jnp.stack(
                [
                    jnp.stack([probe, across(probe, 1, 0)]),
                    jnp.stack([across(probe, 0, far), across(probe, 1, far)]),
                ]
            )
            probes = after(probes, second)
            probes = jnp.concatenate([probes, swapped(probes, "mode", near)], axis=0)
        else:
            object_field = last_part(first, probes, inner, entries)
            probe = jnp.stack([probe, across(probe, 1, 0)])
            probe = jnp.where(parity == 0, probe, probe[::-1]).swapaxes(0, 1).reshape(1, 2, length, length)
    return (object_field, probe)


def solution(mesh):
    placed = (
        P(None, "scan", "mode"),
        P("mode", None, None, None),
        P(("scan", "mode"), None, None),
        P(("scan", "mode"), None),
        P(("scan", "mode")),
    )
    return jax.shard_map(
        local,
        mesh=mesh,
        in_specs=placed,
        out_specs=(P(None, "scan", "mode"), P("mode", None, None, None)),
        check_vma=False,
    )
```

```python
import functools
import math

import jax
import jax.numpy as jnp
import numpy as np
from jax import lax
from jax.experimental import pallas as pl
from jax.experimental.pallas import tpu as pltpu
from jax.sharding import PartitionSpec as P

ITERS = 2
SUBLANES, LANES = 8, 128
F32 = jnp.float32
BF16 = jnp.bfloat16
TABLE = 8


def shifted(value, axis, steps):
    count = lax.axis_size(axis)
    initial, last = (max(0, -steps), min(count, count - steps))
    return lax.ppermute(value, axis, [(source, source + steps) for source in range(initial, last)])


def swapped(value, axis, bit):
    return lax.ppermute(value, axis, [(i, i ^ bit) for i in range(lax.axis_size(axis))])


def paired(value, axis, step, phase):
    lower = [i for i in range(lax.axis_size(axis) - step) if i // step % 2 == phase]
    return lax.ppermute(value, axis, [(i, i + step) for i in lower] + [(i + step, i) for i in lower])


def across(value, scan_bit, mode_bit):
    scans, modes = lax.axis_size("scan"), lax.axis_size("mode")
    other = scan_bit * modes + mode_bit
    return lax.ppermute(value, ("scan", "mode"), [(i, i ^ other) for i in range(scans * modes)])


def after(value, others):
    return lax.optimization_barrier((value, others))[0]


def bits_of(axis):
    return [1 << b for b in range(lax.axis_size(axis).bit_length() - 1)]


def gathered(value, axis):
    for bit in reversed(bits_of(axis)):
        value = jnp.concatenate([value, swapped(value, axis, bit)], axis=0)
    return value


@functools.lru_cache
def fresnel_parts(length):
    ids = np.arange(length, dtype=np.int64)
    phase = ids[:, None] * ids[None, :] % length
    centred = ids - length // 2
    chirp = centred * centred % (4 * length)
    angle = -2.0 * math.pi / length * phase + math.pi / (2 * length) * chirp[None, :]
    real, imag = np.cos(angle) / math.sqrt(length), np.sin(angle) / math.sqrt(length)
    whole = np.block([[real, -imag], [imag, real]])
    parts = []
    for matrix in (whole, whole.T):
        high = matrix.astype(jnp.bfloat16)
        low = (matrix - high.astype(np.float64)).astype(jnp.bfloat16)
        parts.append(np.stack([high, low]))
    return np.stack(parts)


def split(value):
    high = value.astype(BF16)
    return high, (value - high.astype(F32)).astype(BF16)


def dot(a, b):
    return jnp.dot(a, b, preferred_element_type=F32)


def window_of(row, col):
    return (
        pl.multiple_of(row // SUBLANES * SUBLANES, SUBLANES),
        pl.multiple_of(col // LANES * LANES, LANES),
        row % SUBLANES,
        col % LANES,
    )


def cut(wide, down, right, length):
    wide = pltpu.roll(wide, 2 * LANES - right, 1)[:, :length]
    return pltpu.roll(wide, length + SUBLANES - down, 0)[:length]


def placed_in(term, down, right):
    tall = jnp.concatenate([term, jnp.zeros((SUBLANES, term.shape[1]), F32)], axis=0)
    tall = pltpu.roll(pltpu.roll(tall, down, 0), right, 1)
    first = lax.broadcasted_iota(jnp.int32, tall.shape, 1) >= right
    return jnp.concatenate([jnp.where(first, tall, 0.0), jnp.where(first, 0.0, tall)], axis=1)


def patches_kernel(place, first, second, third, patch, density, extended):
    slots, _, length, _ = patch.shape
    rows = first.shape[1]
    for step, tile in enumerate((first, second, third)):
        extended[:, step * rows : (step + 1) * rows] = tile[...]
    total = None
    for slot in range(slots):
        row, col, used = place[3 * slot], place[3 * slot + 1], place[3 * slot + 2]
        top, left, down, right = window_of(row, col)
        here = 0.0
        for part in range(2):
            wide = extended[part, pl.ds(top, length + SUBLANES), pl.ds(left, 2 * LANES)]
            window = cut(wide, down, right, length)
            patch[slot, part] = window
            here = here + window * window
        here = here * used.astype(F32)
        total = here if total is None else total + here
    density[...] = total


def whole_probe(probes, k, part, parity):
    return jnp.concatenate([probes[k, parity, part], probes[k, 1 - parity, part]], axis=0)


def wave_kernel(place, me, patch, density, probes, amplitude, table, windows, *rest):
    (kept, sent, *terms), (sums, x_hi, x_lo, y_hi, y_lo, far, own_probe) = rest[:-7], rest[-7:]
    slots, _, length, _ = patch.shape
    modes = probes.shape[0]
    half = length // 2
    scan = me[0]
    parity = scan % 2

    def from_left(which):
        for pair in range(modes // 2):
            cols = slice(2 * pair * length, 2 * (pair + 1) * length)
            hi, lo = x_hi[:, cols], x_lo[:, cols]
            out = dot(table[which, 0], hi) + dot(table[which, 0], lo) + dot(table[which, 1], hi)
            hi, lo = split(out)
            for k in range(2):
                rows = slice((2 * pair + k) * length, (2 * pair + k + 1) * length)
                cols = slice(k * length, (k + 1) * length)
                y_hi[rows, :length], y_hi[rows, length:] = hi[:length, cols], hi[length:, cols]
                y_lo[rows, :length], y_lo[rows, length:] = lo[:length, cols], lo[length:, cols]

    def from_right(which, k):
        rows = slice(k * length, (k + 1) * length)
        hi, lo = y_hi[rows], y_lo[rows]
        return dot(hi, table[which, 0]) + dot(lo, table[which, 0]) + dot(hi, table[which, 1])

    def set_columns(k, real, imag):
        cols = slice(k * length, (k + 1) * length)
        hi, lo = split(real)
        x_hi[:length, cols], x_lo[:length, cols] = hi, lo
        hi, lo = split(imag)
        x_hi[length:, cols], x_lo[length:, cols] = hi, lo

    sums[...] = jnp.zeros_like(sums)
    for k in range(modes):
        for part in range(2):
            own_probe[k, part] = whole_probe(probes, k, part, parity)
    for slot in range(slots):
        row, col, used = place[3 * slot], place[3 * slot + 1], place[3 * slot + 2].astype(F32)
        obj_re, obj_im = patch[slot, 0], patch[slot, 1]
        for k in range(modes):
            pr, pi = own_probe[k, 0], own_probe[k, 1]
            set_columns(k, pr * obj_re - pi * obj_im, pr * obj_im + pi * obj_re)
        from_left(0)
        intensity = 0.0
        for k in range(modes):
            wave = from_right(1, k)
            far[k] = wave
            square = wave * wave
            intensity = intensity + square[:, :length] + square[:, length:]
        factor = amplitude[slot] / jnp.sqrt(jnp.maximum(intensity, 1.0))
        for k in range(modes):
            set_columns(k, far[k, :, :length] * factor, far[k, :, length:] * factor)
        from_left(1)
        num_re, num_im = 0.0, 0.0
        for k in range(modes):
            near = from_right(0, k)
            pr, pi = own_probe[k, 0], own_probe[k, 1]
            change_re = (near[:, :length] - (pr * obj_re - pi * obj_im)) * used
            change_im = (near[:, length:] - (pr * obj_im + pi * obj_re)) * used
            num_re = num_re + (pr * change_re + pi * change_im)
            num_im = num_im + (pr * change_im - pi * change_re)
            grad_re = obj_re * change_re + obj_im * change_im
            grad_im = obj_re * change_im - obj_im * change_re
            out, at = (kept, k) if k < modes // 2 else (sent, k - modes // 2)
            for part, grad in enumerate((grad_re, grad_im)):
                for top in range(2):
                    where = (at, parity ^ top, slice(part * half, (part + 1) * half))
                    piece = grad[top * half : (top + 1) * half]
                    out[where] = piece if slot == 0 else out[where] + piece
        top, left, down, right = window_of(row, col)
        for part, term in enumerate((num_re, num_im)):
            sums[part, pl.ds(top, length + SUBLANES), pl.ds(left, 2 * LANES)] += placed_in(term, down, right)
    for out in (kept, sent):
        for at in range(modes // 2):
            for top in range(2):
                out[at, parity ^ top, 2 * half :] = density[top * half : (top + 1) * half]
    data_rows = terms[0].shape[0] - windows.shape[0]
    tile_rows = data_rows // 2
    for step, out in enumerate(terms):
        for part in range(2):
            out[part * tile_rows : (part + 1) * tile_rows] = sums[part, step * tile_rows : (step + 1) * tile_rows]
        out[data_rows:] = jnp.zeros((windows.shape[0], out.shape[1]), F32)
        out[data_rows:, LANES : 2 * LANES] = windows[...]


def weight_of(table, me, probes, grid, scan_steps, mode_steps, rows, cols, tile_rows, band_cols, acc):
    modes, length = probes.shape[0], probes.shape[-1]
    above, left = (acc.shape[0] - rows - length, acc.shape[1] - cols - length)
    scan, mode = me[0], me[1]
    power = 0.0
    for k in range(modes):
        real, imag = (whole_probe(probes, k, part, scan % 2) for part in range(2))
        power = power + (real * real + imag * imag)
    acc[...] = jnp.zeros_like(acc)
    for ds in scan_steps:
        for dm in mode_steps:
            inside = (scan + ds >= 0) & (scan + ds < grid[0]) & (mode + dm >= 0) & (mode + dm < grid[1])
            first = jnp.where(inside, (scan + ds) * grid[1] + mode + dm, 0) * TABLE
            for slot in range(TABLE // 3):
                row = table[first + 3 * slot] - scan * tile_rows
                col = table[first + 3 * slot + 1] - mode * band_cols
                used = inside & (table[first + 3 * slot + 2] > 0)
                used &= (row > -length) & (row < rows) & (col > -length) & (col < cols)

                @pl.when(used)
                def _():
                    top, before, down, right = window_of(row + above, col + left)
                    acc[pl.ds(top, length + SUBLANES), pl.ds(before, 2 * LANES)] += placed_in(power, down, right)

    return acc[pl.ds(above, rows), pl.ds(left, cols)] + 1.0


def join_kernel(band_cols, me, inner, outer, entries, from_a, from_b, new_inner, new_outer, for_a, for_b):
    data_rows = inner.shape[0]
    rim = for_a.shape[1]
    lower = (me[0] // 2 % 2 == 0).astype(F32)
    even = (me[1] % 2 == 0).astype(F32)
    a, b = from_a[:data_rows], from_b[:data_rows]
    tiles = (inner[...] + b * lower + a * (1.0 - lower), outer[...] + a * lower + b * (1.0 - lower))
    new_inner[...], new_outer[...] = tiles
    for at, tile in enumerate(tiles):
        rows = slice(at * data_rows, (at + 1) * data_rows)
        left, right = tile[:, :rim], tile[:, band_cols:]
        for_a[rows] = right * even + left * (1.0 - even)
        for_b[rows] = left * even + right * (1.0 - even)
    rest = entries[...] + from_a[data_rows:, LANES : 2 * LANES] + from_b[data_rows:, LANES : 2 * LANES]
    for_a[2 * data_rows :] = rest
    for_b[2 * data_rows :] = rest


def inner_kernel(grid, band_cols, table, me, first, third, probes, inner, outer, from_a, from_b, new_first, new_third, passed, acc):
    _, tile_rows, cols = first.shape
    rim = from_a.shape[1]
    scan, mode = me[0], me[1]
    weight = weight_of(
        table, me, probes, grid, range(-2, 3), range(-1, 2), 3 * tile_rows, cols, tile_rows, band_cols, acc
    )
    inside = jnp.where(lax.broadcasted_iota(jnp.int32, (tile_rows, cols), 1) < (grid[1] - mode) * band_cols, 1.0, 0.0)
    beyond = inside * (scan + 2 < grid[0]).astype(F32)
    is_first = (scan % 2).astype(F32)
    even = (mode % 2 == 0).astype(F32)
    for part in range(2):
        updated = []
        for at, (term, tile, keep) in enumerate(((inner, first, inside), (outer, third, beyond))):
            a, b = (ref[slice((2 * at + part) * tile_rows, (2 * at + part + 1) * tile_rows)] for ref in (from_a, from_b))
            left, right = b * even + a * (1.0 - even), a * even + b * (1.0 - even)
            term = term[part * tile_rows : (part + 1) * tile_rows]
            term = jnp.concatenate([term[:, :rim] + left, term[:, rim:band_cols], term[:, band_cols:] + right], axis=1)
            updated.append(tile[part] + keep * term / weight[2 * at * tile_rows : (2 * at + 1) * tile_rows])
        new_first[part], new_third[part] = updated
        passed[part] = updated[0] * is_first + updated[1] * (1.0 - is_first)


def last_kernel(grid, table, me, probes, weight, acc):
    rows, cols = weight.shape
    weight[...] = weight_of(table, me, probes, grid, range(-2, 1), range(-1, 1), rows, cols, rows, cols, acc)


VMEM = pl.BlockSpec(memory_space=pltpu.VMEM)
SMEM = pl.BlockSpec(memory_space=pltpu.SMEM)


def call(kernel, out_shape, in_specs, scratch=(), flops=0, moved=0):
    return pl.pallas_call(
        kernel,
        out_shape=out_shape,
        in_specs=in_specs,
        out_specs=jax.tree.map(lambda _: VMEM, out_shape),
        scratch_shapes=list(scratch),
        compiler_params=pltpu.CompilerParams(vmem_limit_bytes=16 * 2**20),
        cost_estimate=pl.CostEstimate(flops=flops, bytes_accessed=moved, transcendentals=0),
    )


def local(object_field, probe, amplitude, offsets, counts):
    tile_rows, band_cols = object_field.shape[1:]
    scans, modes = lax.axis_size("scan"), lax.axis_size("mode")
    scan, mode = lax.axis_index("scan"), lax.axis_index("mode")
    length = probe.shape[2]
    slots = amplitude.shape[0]
    reach = -(-length // tile_rows)
    ext_rows, ext_cols = tile_rows + length, band_cols + length
    table = jnp.asarray(fresnel_parts(length))
    used = (jnp.arange(slots, dtype=jnp.int32) < counts[0]).astype(jnp.int32)
    corner = jnp.stack([scan * tile_rows, mode * band_cols]).astype(jnp.int32)
    place = jnp.concatenate([offsets - corner, used[:, None]], axis=1).reshape(-1)

    me = jnp.stack([scan, mode]).astype(jnp.int32)
    parity = scan % 2
    near, far = bits_of("mode")
    half = length // 2

    entry = jnp.concatenate([offsets, used[:, None]], axis=1).reshape(-1)
    entry = jnp.pad(entry, (0, TABLE - entry.shape[0])).astype(F32)
    table_rows = -(-scans * modes * TABLE // (SUBLANES * LANES)) * SUBLANES
    blocks = jnp.arange(table_rows * LANES // TABLE)
    windows = jnp.where((blocks == scan * modes + mode)[:, None], entry[None, :], 0.0).reshape(-1, LANES)
    data_rows = 2 * tile_rows
    even, odd = (parity == 0).astype(F32), (parity == 1).astype(F32)
    even_mode = (mode % 2 == 0).astype(F32)
    lower = (scan // 2 % 2 == 0).astype(F32)

    def sds(*shape):
        return jax.ShapeDtypeStruct(shape, F32)

    def as_halves(value):
        value = value.reshape(value.shape[0], 2, 2, half, length).swapaxes(1, 2)
        return jnp.where(parity == 0, value, value[:, ::-1])

    def scratch(rows, cols):
        return [pltpu.VMEM((reach * tile_rows + rows + length, band_cols + cols + length), F32)]

    def joined_rows(terms):
        arrived = swapped(terms[1], "scan", 1)
        inner = terms[0][:data_rows] + arrived[:data_rows] * odd
        outer = terms[2][:data_rows] + arrived[:data_rows] * even
        entries = terms[0][data_rows:] + arrived[data_rows:]
        b = paired(jnp.concatenate([inner * lower + outer * (1.0 - lower), entries]), "scan", 2, 1)
        a = paired(jnp.concatenate([outer * lower + inner * (1.0 - lower), entries]), "scan", 2, 0)
        rows = 2 * data_rows + table_rows
        return call(
            functools.partial(join_kernel, band_cols),
            [sds(data_rows, ext_cols)] * 2 + [sds(rows, length)] * 2,
            [SMEM] + [VMEM] * 5,
            flops=2**20,
            moved=2**20,
        )(me, inner, outer, entries[:, LANES : 2 * LANES], a, b)

    def inner_update(first, third, probes, inner, outer, for_a, for_b):
        b = paired(for_b, "mode", 1, 1)
        a = paired(for_a, "mode", 1, 0)
        entries = (for_a + a + b)[2 * data_rows :].astype(jnp.int32).reshape(-1)
        first, third, passed = call(
            functools.partial(inner_kernel, (scans, modes), band_cols),
            [sds(2, tile_rows, ext_cols)] * 3,
            [SMEM, SMEM] + [VMEM] * 7,
            scratch(3 * tile_rows, ext_cols),
            flops=2**20,
            moved=2**20,
        )(entries, me, first, third, probes, inner, outer, a, b)
        return first, third, passed, entries

    def with_margin(term, margin):
        return jnp.concatenate([term[:, :length] + margin, term[:, length:band_cols]], axis=1)

    def last_update(terms):
        terms = [term[:data_rows] for term in terms]
        margin = shifted(jnp.concatenate([term[:, band_cols:] for term in terms]), "mode", 1)
        terms = [with_margin(term, margin[i * data_rows : (i + 1) * data_rows]) for i, term in enumerate(terms)]
        arrived = swapped(terms[1], "scan", 1)
        return terms[0] + arrived * odd, terms[2] + arrived * even

    def last_part(tile, probes, terms, entries):
        weight = call(
            functools.partial(last_kernel, (scans, modes)),
            sds(tile_rows, band_cols),
            [SMEM, SMEM, VMEM],
            scratch(tile_rows, band_cols),
            flops=2**20,
            moved=2**20,
        )(entries, me, probes)
        return tile[:, :, :band_cols] + terms.reshape(2, tile_rows, band_cols) / weight

    probes = as_halves(probe)
    probes = jnp.concatenate([probes, swapped(probes, "mode", far)], axis=0)
    tiles = [object_field, shifted(object_field, "scan", -1), shifted(object_field, "scan", -2)]
    tiles = jnp.concatenate(tiles, axis=1)
    tiles = jnp.concatenate([tiles, shifted(tiles[:, :, :length], "mode", -1)], axis=2)
    probes = after(probes, tiles)
    probes = jnp.concatenate([probes, swapped(probes, "mode", near)], axis=0)
    first, second, third = (tiles[:, step * tile_rows : (step + 1) * tile_rows] for step in range(3))
    for iteration in range(ITERS):
        last = iteration == ITERS - 1
        patch, density = call(
            patches_kernel,
            (sds(slots, 2, length, length), sds(length, length)),
            [SMEM] + [VMEM] * 3,
            [pltpu.VMEM((2, ext_rows, ext_cols), F32)],
            flops=2**20,
            moved=2**20,
        )(place, first, second, third)
        rows_out = data_rows + table_rows
        kept, sent, *terms = call(
            wave_kernel,
            (*[sds(modes // 2, 2, 3 * half, length)] * 2, *[sds(rows_out, ext_cols)] * 3),
            [SMEM, SMEM] + [VMEM] * 6,
            [pltpu.VMEM((2, ext_rows, ext_cols), F32)]
            + [pltpu.VMEM((2 * length, modes * length), BF16)] * 2
            + [pltpu.VMEM((modes * length, 2 * length), BF16)] * 2
            + [pltpu.VMEM((modes, length, 2 * length), F32), pltpu.VMEM((modes, 2, length, length), F32)],
            flops=slots * modes * 4 * 3 * 2 * 4 * length**3,
            moved=4 * 2**20,
        )(place, me, patch, density, probes, amplitude, table, windows)
        kept = kept + swapped(sent, "mode", near)
        if last:
            kept, terms = lax.optimization_barrier((kept, terms))
        pass
        own = kept[0, 0] + across(kept[0, 1], 1, 0) + across(kept[1, 0], 0, far) + across(kept[1, 1], 1, far)
        if not last:
            joined = joined_rows(terms)
        pass
        for bit in bits_of("scan")[1:]:
            own = own + swapped(own, "scan", bit)
            pass
        if not last:
            first, third, passed, entries = inner_update(first, third, probes, *joined)
        else:
            inner, outer = last_update(terms)
            inner = inner + shifted(outer, "scan", 2)
        probe = probes[0, 0] + own[: 2 * half].reshape(2, half, length) / (own[2 * half :] + 1.0)
        if not last:
            second = swapped(passed, "scan", 1)
            probes = jnp.stack(
                [
                    jnp.stack([probe, across(probe, 1, 0)]),
                    jnp.stack([across(probe, 0, far), across(probe, 1, far)]),
                ]
            )
            probes = after(probes, second)
            probes = jnp.concatenate([probes, swapped(probes, "mode", near)], axis=0)
        else:
            object_field = last_part(first, probes, inner, entries)
            probe = jnp.stack([probe, across(probe, 1, 0)])
            probe = jnp.where(parity == 0, probe, probe[::-1]).swapaxes(0, 1).reshape(1, 2, length, length)
    return (object_field, probe)


def solution(mesh):
    placed = (
        P(None, "scan", "mode"),
        P("mode", None, None, None),
        P(("scan", "mode"), None, None),
        P(("scan", "mode"), None),
        P(("scan", "mode")),
    )
    return jax.shard_map(
        local,
        mesh=mesh,
        in_specs=placed,
        out_specs=(P(None, "scan", "mode"), P("mode", None, None, None)),
        check_vma=False,
    )
```
